32 devices in a mesh: stream: 2 (over x), expert: 16 (over z, y, core).
Axes of the slice: x: 2, y: 2, z: 4, core: 2. Of those that a mesh axis runs over, the one named last changes fastest.
Arguments:
- tokens: bfloat16 [2048, 2048], P(('stream', 'expert')), may hold values from -6 to 6
- route_gates: float32 [2048, 8], P(('stream', 'expert')), may hold values from 0.1 to 1
- expert_ids: int32 [2048, 8], P(('stream', 'expert')), may hold values from 0 to 15, as said below
- slot_index: int32 [2048, 8], P(('stream', 'expert')), may hold values from -1 to 31, as said below
- gate_quant: bfloat16 [16, 2048, 1024], P('expert', None, 'stream'), may hold values from -0.125 to 0.125
- up_quant: bfloat16 [16, 2048, 1024], P('expert', None, 'stream'), may hold values from -0.125 to 0.125
- down_quant: bfloat16 [16, 2048, 1024], P('expert', None, 'stream'), may hold values from -0.1875 to 0.1875
- gate_scale: float32 [16, 16, 8], P('expert', None, 'stream'), may hold values from 0.5 to 2
- up_scale: float32 [16, 16, 8], P('expert', None, 'stream'), may hold values from 0.5 to 2
- down_scale: float32 [16, 16, 8], P('expert', None, 'stream'), may hold values from 0.5 to 2
Outputs:
- mixed: bfloat16 [2048, 2048], P(('stream', 'expert'))
The draws below stay inside these ranges and needn't reach their ends.
Inputs may be any that keep to these rules, and one draw needn't show every extreme that they name: `expert_ids`: the 8 ids of one token differ. `slot_index`: among the choices of one device's 64 tokens that name one expert, taken in token order, the first 32 get places 0, 1, ... and the rest get -1. In every draw some expert gets all 32 places from every device.
All inputs are finite; a program needn't handle non-finite values.
Results may differ from the reference program's by a relative error of at most 0.0076.
Values may be sent and summed in bfloat16 or wider, within the bound.
No kernel may reach another device: no remote copies, remote signals or barrier semaphores. Data moves between devices by JAX's collectives and lax.ppermute only.
A program may use at most 64 MiB of HBM per device.

```python
import math
import jax
import jax.numpy as jnp
from jax import lax

D = 2048
FF = 1024
TOP = 8
QB = 128
TOK_DEV = 64
EXPERTS = 16
CAP = 32
TOKENS = 2048


def routing(key):
    block_count = TOKENS // TOK_DEV
    keys = jax.random.split(jax.random.fold_in(key, 11), 6)
    offsets = jax.random.permutation(keys[0], EXPERTS)[:TOP].astype(jnp.int32)
    first_pick = jax.random.randint(keys[1], (block_count, TOK_DEV), 0, EXPERTS)
    second_pick = jax.random.randint(keys[2], (block_count, TOK_DEV), 0, EXPERTS)
    rotation = jax.random.randint(keys[3], (), 0, EXPERTS)
    base_ids = (first_pick * second_pick // EXPERTS + rotation) % EXPERTS
    hot_expert = jax.random.randint(keys[4], (), 0, EXPERTS)
    start_at = jax.random.randint(keys[5], (block_count, 1), 0, TOK_DEV)
    in_block = (jnp.arange(TOK_DEV, dtype=jnp.int32)[None, :] - start_at) % TOK_DEV
    base_ids = jnp.where(in_block < CAP, hot_expert, base_ids)
    chosen = ((base_ids[:, :, None] + offsets[None, None, :]) % EXPERTS).astype(jnp.int32)
    one_hot = (chosen[..., None] == jnp.arange(EXPERTS, dtype=jnp.int32)).astype(jnp.int32)
    per_token = one_hot.sum(axis=2)
    earlier = jnp.cumsum(per_token, axis=1) - per_token
    places = jnp.sum(one_hot * earlier[:, :, None, :], axis=3)
    places = jnp.where(places < CAP, places, -1).astype(jnp.int32)
    return (chosen.reshape(TOKENS, TOP), places.reshape(TOKENS, TOP))


def draw_expert_ids(key, part):
    chosen, places = routing(key)
    return chosen


def draw_slot_index(key, part):
    chosen, places = routing(key)
    return places


def steps_of(key, extent, cuts, low, top_value):
    def one(dim, shards_of):
        steps = jax.random.uniform(jax.random.fold_in(jax.random.fold_in(key, 6), dim), (shards_of,), jnp.float32, low / len(cuts), top_value / len(cuts))
        return jnp.repeat(jnp.exp(steps), extent[dim] // shards_of).reshape((-1,) + (1,) * (len(extent) - dim - 1))

    factor_of = one(*cuts[0])
    for cut in cuts[1:]:
        factor_of = factor_of * one(*cut)
    return factor_of


def bell_draw(rng, extent, width, limit, shards=(), held_as=jnp.bfloat16):
    drawn = width * jax.random.normal(rng, extent, jnp.float32)
    if shards:
        drawn = drawn * steps_of(rng, extent, shards, -0.22, 0.18)
    return jnp.clip(drawn, -limit, limit).astype(held_as)


def setup_inputs(seed: int = 0) -> dict:
    arg_keys = jax.random.split(jax.random.key(seed), 11)
    return {
        "tokens": bell_draw(arg_keys[0], (TOKENS, D), 1.0, 6.0, ((0, 32),)),
        "route_gates": jnp.clip(jnp.exp(math.log(1.0) - 2.3025851 * jax.random.uniform(arg_keys[1], (TOKENS, TOP), jnp.float32) ** steps_of(arg_keys[1], (TOKENS, TOP), ((0, 32),), -0.2, 0.2)), 0.1, 1.0),
        "expert_ids": draw_expert_ids(jax.random.fold_in(arg_keys[10], 71), 0),
        "slot_index": draw_slot_index(jax.random.fold_in(arg_keys[10], 71), 0),
        "gate_quant": bell_draw(arg_keys[4], (EXPERTS, D, FF), D ** -0.5, 0.125, ((0, 16), (2, 2))),
        "up_quant": bell_draw(arg_keys[5], (EXPERTS, D, FF), D ** -0.5, 0.125, ((0, 16), (2, 2))),
        "down_quant": bell_draw(arg_keys[6], (EXPERTS, D, FF), FF ** -0.5, 0.1875, ((0, 16), (2, 2))),
        "gate_scale": jnp.clip(jnp.exp(math.log(2.0) - 1.3862944 * jax.random.uniform(arg_keys[7], (EXPERTS, D // QB, FF // QB), jnp.float32) ** steps_of(arg_keys[7], (EXPERTS, D // QB, FF // QB), ((0, 16), (2, 2)), -0.2, 0.2)), 0.5, 2.0),
        "up_scale": jnp.clip(jnp.exp(math.log(2.0) - 1.3862944 * jax.random.uniform(arg_keys[8], (EXPERTS, D // QB, FF // QB), jnp.float32) ** steps_of(arg_keys[8], (EXPERTS, D // QB, FF // QB), ((0, 16), (2, 2)), -0.2, 0.2)), 0.5, 2.0),
        "down_scale": jnp.clip(jnp.exp(math.log(2.0) - 1.3862944 * jax.random.uniform(arg_keys[9], (EXPERTS, D // QB, FF // QB), jnp.float32) ** steps_of(arg_keys[9], (EXPERTS, D // QB, FF // QB), ((0, 16), (2, 2)), -0.2, 0.2)), 0.5, 2.0),
    }


def dequantize(quant, scales):
    expanded = jnp.repeat(jnp.repeat(scales, QB, axis=0), QB, axis=1)
    return (quant.astype(jnp.float32) * expanded).astype(jnp.bfloat16)


def reference(tokens, route_gates, expert_ids, slot_index, gate_quant, up_quant, down_quant, gate_scale, up_scale, down_scale):
    source_count = TOKENS // TOK_DEV
    token_ids = jnp.arange(TOKENS, dtype=jnp.int32)
    is_kept = slot_index >= 0
    source_dev = token_ids // TOK_DEV
    dump_slot = EXPERTS * source_count * CAP
    position = (expert_ids * source_count + source_dev[:, None]) * CAP + jnp.where(is_kept, slot_index, 0)
    position = jnp.where(is_kept, position, dump_slot).astype(jnp.int32).reshape(-1)
    owners = jnp.broadcast_to(token_ids[:, None], slot_index.shape).reshape(-1)
    row_table = jnp.full((dump_slot + 1,), TOKENS, jnp.int32).at[position].set(owners)
    row_table = jnp.where(jnp.arange(dump_slot + 1) == dump_slot, TOKENS, row_table)
    weight_table = jnp.zeros((dump_slot + 1,), jnp.float32).at[position].set(
        jnp.where(is_kept, route_gates, jnp.float32(0.0)).reshape(-1))
    row_table = row_table[:dump_slot].reshape(EXPERTS, source_count * CAP)
    weight_table = weight_table[:dump_slot].reshape(EXPERTS, source_count * CAP)
    padded = jnp.concatenate([tokens, jnp.zeros((1, D), tokens.dtype)], axis=0)

    def expert_step(running, packed):
        row_ids, weighting, gate_q, up_q, down_q, gate_s, up_s, down_s = packed
        gathered_rows = padded[row_ids]
        w_gate = dequantize(gate_q, gate_s)
        w_up = dequantize(up_q, up_s)
        w_down = dequantize(down_q, down_s)
        gate_act = jnp.dot(gathered_rows, w_gate, preferred_element_type=jnp.float32)
        up_act = jnp.dot(gathered_rows, w_up, preferred_element_type=jnp.float32)
        hidden = (jax.nn.silu(gate_act) * up_act).astype(jnp.bfloat16)
        answer = jnp.dot(hidden, w_down.T, preferred_element_type=jnp.float32).astype(jnp.bfloat16)
        running = running.at[row_ids].add(weighting[:, None] * answer.astype(jnp.float32))
        return running, None

    initial = jnp.zeros((TOKENS + 1, D), jnp.float32)
    running, _ = lax.scan(expert_step, initial, (row_table, weight_table, gate_quant, up_quant, down_quant, gate_scale, up_scale, down_scale))
    return running[:TOKENS].astype(jnp.bfloat16)
```

```python
import functools

import jax
import jax.numpy as jnp
from jax import lax
from jax.experimental import pallas as pl
from jax.experimental.pallas import tpu as pltpu
from jax.sharding import PartitionSpec as P

QB = 128


def dequantize(quant, scales):
    expanded = jnp.repeat(jnp.repeat(scales, QB, axis=0), QB, axis=1)
    return (quant.astype(jnp.float32) * expanded).astype(jnp.bfloat16)


def exchange_rows(
    tokens,
    route_gates,
    expert_ids,
    slot_index,
    gate_quant,
    up_quant,
    down_quant,
    gate_scale,
    up_scale,
    down_scale,
):
    experts = lax.axis_size("expert")
    tok_rows = tokens.shape[0]
    top_count = expert_ids.shape[1]
    width = tokens.shape[1]
    capacity = max(2, tok_rows * top_count // experts)
    row_count = experts * capacity
    is_kept = slot_index >= 0
    position = jnp.where(is_kept, expert_ids * capacity + slot_index, -1)
    selector = jnp.any(
        position[None, :, :] == jnp.arange(row_count, dtype=jnp.int32)[:, None, None], axis=2
    )
    outgoing = jnp.dot(selector.astype(jnp.bfloat16), tokens, preferred_element_type=jnp.float32)
    outgoing = outgoing.astype(jnp.bfloat16).reshape(experts, capacity, width)
    incoming = lax.all_to_all(outgoing, "expert", split_axis=0, concat_axis=0, tiled=True).reshape(
        row_count, width
    )
    w_gate = dequantize(gate_quant[0], gate_scale[0])
    w_up = dequantize(up_quant[0], up_scale[0])
    w_down = dequantize(down_quant[0], down_scale[0])
    gate_piece = lax.all_gather(w_gate, "stream", axis=1, tiled=True)
    up_piece = lax.all_gather(w_up, "stream", axis=1, tiled=True)
    down_piece = lax.all_gather(w_down, "stream", axis=1, tiled=True)
    gate_act = jnp.dot(incoming, gate_piece, preferred_element_type=jnp.float32)
    up_act = jnp.dot(incoming, up_piece, preferred_element_type=jnp.float32)
    hidden = (jax.nn.silu(gate_act) * up_act).astype(jnp.bfloat16)
    running = jnp.einsum("rf,df->rd", hidden, down_piece, preferred_element_type=jnp.float32)
    expert_out = running.astype(jnp.bfloat16).reshape(experts, capacity, width)
    returned = lax.all_to_all(
        expert_out, "expert", split_axis=0, concat_axis=0, tiled=True
    ).reshape(row_count, width)
    gather_at = jnp.where(is_kept, position, 0).reshape(-1)
    picked = jnp.take(returned, gather_at, axis=0).reshape(tok_rows, top_count, width)
    weighting = jnp.where(is_kept, route_gates, jnp.float32(0.0))
    mixed_out = jnp.sum(weighting[:, :, None] * picked.astype(jnp.float32), axis=1)
    return mixed_out.astype(jnp.bfloat16)


AXES = ("stream", "expert")
LANES = 128


def pack_kernel(gates_ref, ids_ref, slots_ref, tokens_ref, out_ref):
    width = tokens_ref.shape[1]
    rows = tokens_ref.shape[0]
    columns = LANES // 2
    weighting = jnp.where(slots_ref[...] >= 0, gates_ref[...], jnp.float32(0.0))
    ids = ids_ref[...]
    column = lax.broadcasted_iota(jnp.int32, (columns, rows), 0)
    spread = jnp.zeros((columns, rows), jnp.float32)
    for k in range(ids.shape[0]):
        spread += jnp.where(ids[k : k + 1] == column, weighting[k : k + 1], jnp.float32(0.0))
    high = spread.astype(jnp.bfloat16).astype(jnp.float32)
    both = jnp.concatenate([high, spread - high], axis=0)
    out_ref[:, :width] = tokens_ref[...]
    out_ref[:, width:] = both.T.astype(jnp.bfloat16)


def pack(tokens, route_gates, expert_ids, slot_index):
    rows, width = tokens.shape
    return pl.pallas_call(
        pack_kernel,
        out_shape=jax.ShapeDtypeStruct((rows, width + LANES), jnp.bfloat16),
        cost_estimate=pl.CostEstimate(
            flops=rows * width, bytes_accessed=4 * rows * width, transcendentals=0
        ),
        name="pack",
    )(route_gates.T, expert_ids.T, slot_index.T, tokens)


def scale_kernel(*refs, pieces):
    scales, quants, out_ref = refs[:3], refs[3:6], refs[6]
    factors, held = refs[7:10], refs[10:13]
    factor_sems, sems = refs[13:]
    width, half = held[0].shape
    rows = width // pieces

    def fetch(which, piece):
        at = pl.ds(piece * rows, rows)
        return pltpu.make_async_copy(
            quants[which].at[0, at], held[which].at[at], sems.at[which, piece]
        )

    factor_copies = [
        pltpu.make_async_copy(scales[i], factors[i], factor_sems.at[i]) for i in range(3)
    ]
    for copy in factor_copies:
        copy.start()
    for piece in range(pieces):
        for which in range(3):
            fetch(which, piece).start()
    for copy in factor_copies:
        copy.wait()

    def work(piece, carry):
        for which in range(3):
            fetch(which, piece).wait()
            for i in range(rows // QB):
                for j in range(half // QB):
                    at = piece * (rows // QB) + i
                    row = pl.ds(pl.multiple_of(at * QB, QB), QB)
                    block = held[which][row, pl.ds(j * QB, QB)].astype(jnp.float32)
                    block = (block * factors[which][j, at]).astype(out_ref.dtype)
                    out_ref[row, pl.ds(which * half + j * QB, QB)] = block
        return carry

    lax.fori_loop(0, pieces, work, 0)


def scale_weights(quants, scales):
    _, width, half = quants[0].shape
    pieces = 8
    scales = [scale[0].T for scale in scales]
    return pl.pallas_call(
        functools.partial(scale_kernel, pieces=pieces),
        in_specs=[pl.BlockSpec(memory_space=pl.ANY)] * 6,
        out_specs=pl.BlockSpec(memory_space=pltpu.VMEM),
        out_shape=pltpu.VMEM((width, 3 * half), jnp.bfloat16),
        scratch_shapes=[pltpu.SMEM(scales[0].shape, jnp.float32)] * 3
        + [pltpu.VMEM((width, half), jnp.bfloat16)] * 3
        + [pltpu.SemaphoreType.DMA((3,)), pltpu.SemaphoreType.DMA((3, pieces))],
        cost_estimate=pl.CostEstimate(
            flops=3 * width * half, bytes_accessed=12 * width * half, transcendentals=0
        ),
        compiler_params=pltpu.CompilerParams(vmem_limit_bytes=52 * 2**20),
        name="scale_weights",
    )(*scales, *quants)


def contract_last(a, b):
    return lax.dot_general(a, b, (((1,), (1,)), ((), ())), preferred_element_type=jnp.float32)


def hidden_units(me, which, rows_ref, weight, width, half):
    columns = rows_ref[:, width:].astype(jnp.float32)
    rank = lax.rem(lax.broadcasted_iota(jnp.int32, columns.shape, 1), LANES // 2)
    gates = jnp.sum(
        jnp.where(rank == me[which], columns, jnp.float32(0.0)), axis=1, keepdims=True
    )
    gate_act = jnp.dot(rows_ref[:, :width], weight[:, :half], preferred_element_type=jnp.float32)
    up_act = jnp.dot(
        rows_ref[:, :width], weight[:, half : 2 * half], preferred_element_type=jnp.float32
    )
    return (gate_act / (1.0 + jnp.exp(-gate_act)) * up_act * gates).astype(jnp.bfloat16)


def hidden_kernel(me_ref, *refs):
    *messages, weight, out_ref, rows_ref = refs
    rows = messages[0].shape[0]
    for i, message in enumerate(messages):
        rows_ref[pl.ds(i * rows, rows), :] = message[...]
    width, half = rows_ref.shape[1] - LANES, out_ref.shape[1]
    out_ref[...] = hidden_units(me_ref, 0, rows_ref, weight, width, half)


def own_hidden(me, messages, weight):
    rows, columns = messages[0].shape
    total = len(messages) * rows
    width, half = columns - LANES, weight.shape[1] // 3
    vmem = pl.BlockSpec(memory_space=pltpu.VMEM)
    return pl.pallas_call(
        hidden_kernel,
        in_specs=[pl.BlockSpec(memory_space=pltpu.SMEM)] + [vmem] * (len(messages) + 1),
        out_specs=vmem,
        out_shape=pltpu.VMEM((total, half), jnp.bfloat16),
        scratch_shapes=[pltpu.VMEM((total, columns), jnp.bfloat16)],
        cost_estimate=pl.CostEstimate(
            flops=4 * total * width * half,
            bytes_accessed=4 * width * half + 2 * total * width,
            transcendentals=total * half,
        ),
        compiler_params=pltpu.CompilerParams(vmem_limit_bytes=20 * 2**20),
        name="own_hidden",
    )(me, *messages, weight)


def expert_kernel(me_ref, *refs, blocks, fetch, begun):
    refs = list(refs)

    def take(count):
        taken = refs[:count]
        del refs[:count]
        return taken

    messages = take(blocks)
    mine, other = take(2)
    before = take(1) if begun else []
    outs = take(blocks)
    kept = take(1) if fetch else []
    rows_ref, *sems = refs
    rows, width = outs[0].shape
    half = mine.shape[1] // 3
    copies = []
    if fetch:
        for part in range(3):
            at = pl.ds(part * half, half)
            source, target = other.at[:, at], kept[0].at[:, at]
            copies.append(pltpu.make_async_copy(source, target, sems[0].at[part]))
        other = kept[0]
    for copy in copies:
        copy.start()
    for i, message in enumerate(messages):
        rows_ref[pl.ds(i * rows, rows), :] = message[...]
    if begun:
        first = before[0][...]
    else:
        first = hidden_units(me_ref, 0, rows_ref, mine, width, half)
    for copy in copies:
        copy.wait()
    second = hidden_units(me_ref, 1, rows_ref, other, width, half)
    for j in range(width // half):
        at = pl.ds(j * half, half)
        answer = contract_last(first, mine[at, 2 * half :])
        answer += contract_last(second, other[at, 2 * half :])
        for i in range(blocks):
            outs[i][:, at] = answer[i * rows : (i + 1) * rows].astype(outs[i].dtype)


def run_experts(me, messages, mine, other, before=None, fetch=False):
    rows, columns = messages[0].shape
    width, half = columns - LANES, mine.shape[1] // 3
    blocks = len(messages)
    total = blocks * rows
    vmem = pl.BlockSpec(memory_space=pltpu.VMEM)
    out_shape = [jax.ShapeDtypeStruct((rows, width), jnp.bfloat16)] * blocks
    scratch_shapes = [pltpu.VMEM((total, columns), jnp.bfloat16)]
    if fetch:
        out_shape.append(pltpu.VMEM(other.shape, jnp.bfloat16))
        scratch_shapes.append(pltpu.SemaphoreType.DMA((3,)))
    others = [] if before is None else [before]
    return list(
        pl.pallas_call(
            functools.partial(
                expert_kernel, blocks=blocks, fetch=fetch, begun=before is not None
            ),
            in_specs=[pl.BlockSpec(memory_space=pltpu.SMEM)]
            + [vmem] * (blocks + 1)
            + [pl.BlockSpec(memory_space=pl.ANY) if fetch else vmem]
            + [vmem] * len(others),
            out_specs=[vmem] * len(out_shape),
            out_shape=out_shape,
            scratch_shapes=scratch_shapes,
            cost_estimate=pl.CostEstimate(
                flops=12 * total * width * half,
                bytes_accessed=12 * width * half + 4 * total * width,
                transcendentals=2 * total * half,
            ),
            compiler_params=pltpu.CompilerParams(vmem_limit_bytes=20 * 2**20),
            name="run_experts",
        )(me, *messages, mine, other, *others)
    )


def hop(value, bit, devices):
    return lax.ppermute(value, AXES, [(i, i ^ bit) for i in range(devices)])


def after(value, *others):
    return lax.optimization_barrier((value, *others))[0]


def add(*terms):
    total = terms[0].astype(jnp.float32)
    for term in terms[1:]:
        total = total + term.astype(jnp.float32)
    return total.astype(jnp.bfloat16)


def gather_tokens(
    tokens,
    route_gates,
    expert_ids,
    slot_index,
    gate_quant,
    up_quant,
    down_quant,
    gate_scale,
    up_scale,
    down_scale,
):
    experts = lax.axis_size("expert")
    devices = experts * lax.axis_size("stream")

    def send(value, bit):
        return hop(value, bit, devices)

    core, y, z1, z2, z3, x = 1, 2, 4, 8, 12, experts
    me = lax.axis_index("expert")
    pair = jnp.stack([me, me ^ 1]).astype(jnp.int32)
    s0 = pack(tokens, route_gates, expert_ids, slot_index)
    s2 = send(s0, z2)
    s1 = send(s0, z1)
    x0 = send(s0, x)
    y0 = send(s0, y)
    mine = scale_weights(
        (gate_quant, up_quant, down_quant), (gate_scale, up_scale, down_scale)
    )
    swapped = send(after(mine, s2, s1, x0, y0), core)
    s3 = send(s2, z1)
    y2 = send(after(s2, y0), y)
    x2 = send(after(s2, x0), x)
    begun = own_hidden(pair, (s0, x0, y0, s1), mine)
    d0 = send(after(x0, y2, s3, begun), y)
    d2 = send(after(y2, x2, s3, begun), x)
    x3 = send(after(s3, x2), x)
    y3 = send(after(s3, y2), y)
    last = (s0, x0, y0, s1)
    s2, s3, x2, y2, swapped = run_experts(pair, (s2, s3, x2, y2), mine, swapped, fetch=True)

    def work(*messages):
        return run_experts(pair, messages, mine, swapped)

    d3 = send(after(x3, s2), y)
    x1 = send(after(s1, x3, d0, s2), x)
    d1 = send(after(d0, s2), z1)
    y1 = send(after(s1, d0, s2), y)
    d2, x3, y3, d0 = work(after(d2, s2), x3, y3, d0)
    bx2 = send(after(x2, d3, x1, d2), x)
    by2 = send(after(y2, d3, x1, d2), y)
    bd2 = send(after(d2, d3, x1, d1), z1)
    d3, x1, y1, d1 = work(after(d3, d2), x1, y1, d1)
    bd3 = send(after(add(d3, bd2), bx2, by2), x)
    bd1 = send(after(d1, bd2, bx2, by2), z1)
    by1 = send(after(y1, bd2, bx2, by2), y)
    bx3 = send(after(x3, bd2, bx2, by2, d3), x)
    bs2 = send(after(add(s2, bx2, by2), bd2, d3), z2)
    by3 = send(add(y3, bd3), y)
    bd0 = send(after(add(d0, bd1), by1), y)
    bx1 = send(after(x1, bd3, by1), x)
    s0, x0, y0, s1 = run_experts(
        pair, (after(last[0], d3, bd3, bd1), *last[1:]), mine, swapped, before=begun
    )
    by0 = send(y0, y)
    bs3 = send(add(s3, bx3, by3), z3)
    bs1 = send(add(s1, bx1, by1), z1)
    bx0 = send(add(x0, bd0), x)
    return add(s0, bx0, by0, bs1, bs2, bs3)


def solution(mesh):
    streams = mesh.shape["stream"]
    experts = mesh.shape["expert"]

    def local(tokens, *rest):
        all_tokens = tokens.size * streams * experts
        weights = 3 * rest[3].size * streams
        move_tokens = (streams, experts) == (2, 16) and all_tokens < weights
        return (gather_tokens if move_tokens else exchange_rows)(tokens, *rest)

    return jax.shard_map(
        local,
        mesh=mesh,
        in_specs=(
            P(("stream", "expert"), None),
            P(("stream", "expert"), None),
            P(("stream", "expert"), None),
            P(("stream", "expert"), None),
            P("expert", None, "stream"),
            P("expert", None, "stream"),
            P("expert", None, "stream"),
            P("expert", None, "stream"),
            P("expert", None, "stream"),
            P("expert", None, "stream"),
        ),
        out_specs=P(("stream", "expert"), None),
        check_vma=False,
    )
```

```python
import functools

import jax
import jax.numpy as jnp
from jax import lax
from jax.experimental import pallas as pl
from jax.experimental.pallas import tpu as pltpu
from jax.sharding import PartitionSpec as P

QB = 128


def dequantize(quant, scales):
    expanded = jnp.repeat(jnp.repeat(scales, QB, axis=0), QB, axis=1)
    return (quant.astype(jnp.float32) * expanded).astype(jnp.bfloat16)


def exchange_rows(
    tokens,
    route_gates,
    expert_ids,
    slot_index,
    gate_quant,
    up_quant,
    down_quant,
    gate_scale,
    up_scale,
    down_scale,
):
    experts = lax.axis_size("expert")
    tok_rows = tokens.shape[0]
    top_count = expert_ids.shape[1]
    width = tokens.shape[1]
    capacity = max(2, tok_rows * top_count // experts)
    row_count = experts * capacity
    is_kept = slot_index >= 0
    position = jnp.where(is_kept, expert_ids * capacity + slot_index, -1)
    selector = jnp.any(
        position[None, :, :] == jnp.arange(row_count, dtype=jnp.int32)[:, None, None], axis=2
    )
    outgoing = jnp.dot(selector.astype(jnp.bfloat16), tokens, preferred_element_type=jnp.float32)
    outgoing = outgoing.astype(jnp.bfloat16).reshape(experts, capacity, width)
    incoming = lax.all_to_all(outgoing, "expert", split_axis=0, concat_axis=0, tiled=True).reshape(
        row_count, width
    )
    w_gate = dequantize(gate_quant[0], gate_scale[0])
    w_up = dequantize(up_quant[0], up_scale[0])
    w_down = dequantize(down_quant[0], down_scale[0])
    gate_piece = lax.all_gather(w_gate, "stream", axis=1, tiled=True)
    up_piece = lax.all_gather(w_up, "stream", axis=1, tiled=True)
    down_piece = lax.all_gather(w_down, "stream", axis=1, tiled=True)
    gate_act = jnp.dot(incoming, gate_piece, preferred_element_type=jnp.float32)
    up_act = jnp.dot(incoming, up_piece, preferred_element_type=jnp.float32)
    hidden = (jax.nn.silu(gate_act) * up_act).astype(jnp.bfloat16)
    running = jnp.einsum("rf,df->rd", hidden, down_piece, preferred_element_type=jnp.float32)
    expert_out = running.astype(jnp.bfloat16).reshape(experts, capacity, width)
    returned = lax.all_to_all(
        expert_out, "expert", split_axis=0, concat_axis=0, tiled=True
    ).reshape(row_count, width)
    gather_at = jnp.where(is_kept, position, 0).reshape(-1)
    picked = jnp.take(returned, gather_at, axis=0).reshape(tok_rows, top_count, width)
    weighting = jnp.where(is_kept, route_gates, jnp.float32(0.0))
    mixed_out = jnp.sum(weighting[:, :, None] * picked.astype(jnp.float32), axis=1)
    return mixed_out.astype(jnp.bfloat16)


AXES = ("stream", "expert")
LANES = 128


def pack_kernel(gates_ref, ids_ref, slots_ref, tokens_ref, out_ref):
    width = tokens_ref.shape[1]
    rows = tokens_ref.shape[0]
    columns = LANES // 2
    weighting = jnp.where(slots_ref[...] >= 0, gates_ref[...], jnp.float32(0.0))
    ids = ids_ref[...]
    column = lax.broadcasted_iota(jnp.int32, (columns, rows), 0)
    spread = jnp.zeros((columns, rows), jnp.float32)
    for k in range(ids.shape[0]):
        spread += jnp.where(ids[k : k + 1] == column, weighting[k : k + 1], jnp.float32(0.0))
    high = spread.astype(jnp.bfloat16).astype(jnp.float32)
    both = jnp.concatenate([high, spread - high], axis=0)
    out_ref[:, :width] = tokens_ref[...]
    out_ref[:, width:] = both.T.astype(jnp.bfloat16)


def pack(tokens, route_gates, expert_ids, slot_index):
    rows, width = tokens.shape
    return pl.pallas_call(
        pack_kernel,
        out_shape=jax.ShapeDtypeStruct((rows, width + LANES), jnp.bfloat16),
        cost_estimate=pl.CostEstimate(
            flops=rows * width, bytes_accessed=4 * rows * width, transcendentals=0
        ),
        name="pack",
    )(route_gates.T, expert_ids.T, slot_index.T, tokens)


def scale_kernel(*refs, pieces):
    scales, quants, out_ref = refs[:3], refs[3:6], refs[6]
    factors, held = refs[7:10], refs[10:13]
    factor_sems, sems = refs[13:]
    width, half = held[0].shape
    rows = width // pieces

    def fetch(which, piece):
        at = pl.ds(piece * rows, rows)
        return pltpu.make_async_copy(
            quants[which].at[0, at], held[which].at[at], sems.at[which, piece]
        )

    factor_copies = [
        pltpu.make_async_copy(scales[i], factors[i], factor_sems.at[i]) for i in range(3)
    ]
    for copy in factor_copies:
        copy.start()
    for piece in range(pieces):
        for which in range(3):
            fetch(which, piece).start()
    for copy in factor_copies:
        copy.wait()

    def work(piece, carry):
        for which in range(3):
            fetch(which, piece).wait()
            for i in range(rows // QB):
                for j in range(half // QB):
                    at = piece * (rows // QB) + i
                    row = pl.ds(pl.multiple_of(at * QB, QB), QB)
                    block = held[which][row, pl.ds(j * QB, QB)].astype(jnp.float32)
                    block = (block * factors[which][j, at]).astype(out_ref.dtype)
                    out_ref[row, pl.ds(which * half + j * QB, QB)] = block
        return carry

    lax.fori_loop(0, pieces, work, 0)


def scale_weights(quants, scales):
    _, width, half = quants[0].shape
    pieces = 8
    scales = [scale[0].T for scale in scales]
    return pl.pallas_call(
        functools.partial(scale_kernel, pieces=pieces),
        in_specs=[pl.BlockSpec(memory_space=pl.ANY)] * 6,
        out_specs=pl.BlockSpec(memory_space=pltpu.VMEM),
        out_shape=pltpu.VMEM((width, 3 * half), jnp.bfloat16),
        scratch_shapes=[pltpu.SMEM(scales[0].shape, jnp.float32)] * 3
        + [pltpu.VMEM((width, half), jnp.bfloat16)] * 3
        + [pltpu.SemaphoreType.DMA((3,)), pltpu.SemaphoreType.DMA((3, pieces))],
        cost_estimate=pl.CostEstimate(
            flops=3 * width * half, bytes_accessed=12 * width * half, transcendentals=0
        ),
        compiler_params=pltpu.CompilerParams(vmem_limit_bytes=52 * 2**20),
        name="scale_weights",
    )(*scales, *quants)


def contract_last(a, b):
    return lax.dot_general(a, b, (((1,), (1,)), ((), ())), preferred_element_type=jnp.float32)


def hidden_units(me, which, rows_ref, weight, width, half):
    columns = rows_ref[:, width:].astype(jnp.float32)
    rank = lax.rem(lax.broadcasted_iota(jnp.int32, columns.shape, 1), LANES // 2)
    gates = jnp.sum(
        jnp.where(rank == me[which], columns, jnp.float32(0.0)), axis=1, keepdims=True
    )
    gate_act = jnp.dot(rows_ref[:, :width], weight[:, :half], preferred_element_type=jnp.float32)
    up_act = jnp.dot(
        rows_ref[:, :width], weight[:, half : 2 * half], preferred_element_type=jnp.float32
    )
    return (gate_act / (1.0 + jnp.exp(-gate_act)) * up_act * gates).astype(jnp.bfloat16)


def expert_kernel(me_ref, *refs, blocks, fetch):
    refs = list(refs)

    def take(count):
        taken = refs[:count]
        del refs[:count]
        return taken

    messages = take(blocks)
    mine, other = take(2)
    kept = None
    if fetch:
        *outs, kept, rows_ref, sem = refs
        copy = pltpu.make_async_copy(other, kept, sem)
        copy.start()
        other = kept
    else:
        *outs, rows_ref = refs
    width = outs[0].shape[1]
    half = mine.shape[1] // 3
    row = 0
    for message in messages:
        rows_ref[pl.ds(row, message.shape[0]), :] = message[...]
        row += message.shape[0]
    first = hidden_units(me_ref, 0, rows_ref, mine, width, half)
    if fetch:
        copy.wait()
    second = hidden_units(me_ref, 1, rows_ref, other, width, half)
    for j in range(width // half):
        at = pl.ds(j * half, half)
        answer = contract_last(first, mine[at, 2 * half :])
        answer += contract_last(second, other[at, 2 * half :])
        row = 0
        for out in outs:
            out[:, at] = answer[row : row + out.shape[0]].astype(out.dtype)
            row += out.shape[0]


def run_experts(me, messages, mine, other, rows_out, fetch=False):
    columns = messages[0].shape[1]
    width, half = columns - LANES, mine.shape[1] // 3
    total = sum(message.shape[0] for message in messages)
    vmem = pl.BlockSpec(memory_space=pltpu.VMEM)
    out_shape = [jax.ShapeDtypeStruct((n, width), jnp.bfloat16) for n in rows_out]
    scratch_shapes = [pltpu.VMEM((total, columns), jnp.bfloat16)]
    if fetch:
        out_shape.append(pltpu.VMEM(other.shape, jnp.bfloat16))
        scratch_shapes.append(pltpu.SemaphoreType.DMA)
    return list(
        pl.pallas_call(
            functools.partial(expert_kernel, blocks=len(messages), fetch=fetch),
            in_specs=[pl.BlockSpec(memory_space=pltpu.SMEM)]
            + [vmem] * (len(messages) + 1)
            + [pl.BlockSpec(memory_space=pl.ANY) if fetch else vmem],
            out_specs=[vmem] * len(out_shape),
            out_shape=out_shape,
            scratch_shapes=scratch_shapes,
            cost_estimate=pl.CostEstimate(
                flops=12 * total * width * half,
                bytes_accessed=12 * width * half + 4 * total * width,
                transcendentals=2 * total * half,
            ),
            compiler_params=pltpu.CompilerParams(vmem_limit_bytes=24 * 2**20),
            name="run_experts",
        )(me, *messages, mine, other)
    )


def hop(value, bit, devices):
    return lax.ppermute(value, AXES, [(i, i ^ bit) for i in range(devices)])


def after(value, *others):
    return lax.optimization_barrier((value, *others))[0]


def add(*terms):
    total = terms[0].astype(jnp.float32)
    for term in terms[1:]:
        total = total + term.astype(jnp.float32)
    return total.astype(jnp.bfloat16)


def gather_tokens(
    tokens,
    route_gates,
    expert_ids,
    slot_index,
    gate_quant,
    up_quant,
    down_quant,
    gate_scale,
    up_scale,
    down_scale,
):
    experts = lax.axis_size("expert")
    devices = experts * lax.axis_size("stream")

    def send(value, bit):
        return hop(value, bit, devices)

    core, y, z1, z2, z3, x = 1, 2, 4, 8, 12, experts
    me = lax.axis_index("expert")
    pair = jnp.stack([me, me ^ 1]).astype(jnp.int32)
    s0 = pack(tokens, route_gates, expert_ids, slot_index)
    s2 = send(s0, z2)
    x0 = send(s0, x)
    y0 = send(s0, y)
    mine = scale_weights(
        (gate_quant, up_quant, down_quant), (gate_scale, up_scale, down_scale)
    )
    swapped = send(after(mine, s2, x0, y0), core)
    s13 = send(jnp.concatenate([s0, s2]), z1)
    y2 = send(after(s2, y0), y)
    x2 = send(after(s2, x0), x)
    d0 = send(after(x0, s2), y)
    d2 = send(after(y2, x2), x)
    x13 = send(after(s13, x2), x)
    y13 = send(after(s13, y2), y)
    d13 = send(jnp.concatenate([d0, d2]), z1)
    rows = s0.shape[0]
    x02, y02, d02, s0, s2, swapped = run_experts(
        pair,
        (x0, x2, y0, y2, d0, d2, s0, s2),
        mine,
        swapped,
        (2 * rows, 2 * rows, 2 * rows, rows, rows),
        fetch=True,
    )
    bx02 = send(after(x02, x13, y13), x)
    by02 = send(after(y02, x13, y13), y)
    bd02 = send(after(d02, d13), z1)
    d1, d3, x1, x3, y1, y3, s1, s3 = run_experts(
        pair, (after(d13, d02), x13, y13, s13), mine, swapped, (rows,) * 8
    )
    bd3 = send(after(add(d3, bd02[rows:]), bx02, by02), x)
    bd1 = send(after(add(d1, bd02[:rows]), bx02, by02), y)
    bs2 = send(after(add(s2, bx02[rows:], by02[rows:]), bd02, s3), z2)
    by1 = send(after(y1, bx02, by02, bd02), y)
    bx3 = send(after(x3, bd3), x)
    by3 = send(add(y3, bd3), y)
    bx1 = send(after(add(x1, bd1), bd3, bx3), x)
    bs3 = send(add(s3, bx3, by3), z3)
    bs1 = send(add(s1, bx1, by1), z1)
    return add(s0, bx02[:rows], by02[:rows], bs1, bs2, bs3)


def solution(mesh):
    streams = mesh.shape["stream"]
    experts = mesh.shape["expert"]

    def local(tokens, *rest):
        all_tokens = tokens.size * streams * experts
        weights = 3 * rest[3].size * streams
        move_tokens = (streams, experts) == (2, 16) and all_tokens < weights
        return (gather_tokens if move_tokens else exchange_rows)(tokens, *rest)

    return jax.shard_map(
        local,
        mesh=mesh,
        in_specs=(
            P(("stream", "expert"), None),
            P(("stream", "expert"), None),
            P(("stream", "expert"), None),
            P(("stream", "expert"), None),
            P("expert", None, "stream"),
            P("expert", None, "stream"),
            P("expert", None, "stream"),
            P("expert", None, "stream"),
            P("expert", None, "stream"),
            P("expert", None, "stream"),
        ),
        out_specs=P(("stream", "expert"), None),
        check_vma=False,
    )
```

```python
import functools

import jax
import jax.numpy as jnp
from jax import lax
from jax.experimental import pallas as pl
from jax.experimental.pallas import tpu as pltpu
from jax.sharding import PartitionSpec as P

QB = 128


def dequantize(quant, scales):
    expanded = jnp.repeat(jnp.repeat(scales, QB, axis=0), QB, axis=1)
    return (quant.astype(jnp.float32) * expanded).astype(jnp.bfloat16)


def exchange_rows(
    tokens,
    route_gates,
    expert_ids,
    slot_index,
    gate_quant,
    up_quant,
    down_quant,
    gate_scale,
    up_scale,
    down_scale,
):
    experts = lax.axis_size("expert")
    tok_rows = tokens.shape[0]
    top_count = expert_ids.shape[1]
    width = tokens.shape[1]
    capacity = max(2, tok_rows * top_count // experts)
    row_count = experts * capacity
    is_kept = slot_index >= 0
    position = jnp.where(is_kept, expert_ids * capacity + slot_index, -1)
    selector = jnp.any(
        position[None, :, :] == jnp.arange(row_count, dtype=jnp.int32)[:, None, None], axis=2
    )
    outgoing = jnp.dot(selector.astype(jnp.bfloat16), tokens, preferred_element_type=jnp.float32)
    outgoing = outgoing.astype(jnp.bfloat16).reshape(experts, capacity, width)
    incoming = lax.all_to_all(outgoing, "expert", split_axis=0, concat_axis=0, tiled=True).reshape(
        row_count, width
    )
    w_gate = dequantize(gate_quant[0], gate_scale[0])
    w_up = dequantize(up_quant[0], up_scale[0])
    w_down = dequantize(down_quant[0], down_scale[0])
    gate_piece = lax.all_gather(w_gate, "stream", axis=1, tiled=True)
    up_piece = lax.all_gather(w_up, "stream", axis=1, tiled=True)
    down_piece = lax.all_gather(w_down, "stream", axis=1, tiled=True)
    gate_act = jnp.dot(incoming, gate_piece, preferred_element_type=jnp.float32)
    up_act = jnp.dot(incoming, up_piece, preferred_element_type=jnp.float32)
    hidden = (jax.nn.silu(gate_act) * up_act).astype(jnp.bfloat16)
    running = jnp.einsum("rf,df->rd", hidden, down_piece, preferred_element_type=jnp.float32)
    expert_out = running.astype(jnp.bfloat16).reshape(experts, capacity, width)
    returned = lax.all_to_all(
        expert_out, "expert", split_axis=0, concat_axis=0, tiled=True
    ).reshape(row_count, width)
    gather_at = jnp.where(is_kept, position, 0).reshape(-1)
    picked = jnp.take(returned, gather_at, axis=0).reshape(tok_rows, top_count, width)
    weighting = jnp.where(is_kept, route_gates, jnp.float32(0.0))
    mixed_out = jnp.sum(weighting[:, :, None] * picked.astype(jnp.float32), axis=1)
    return mixed_out.astype(jnp.bfloat16)


AXES = ("stream", "expert")
LANES = 128


def pack_kernel(gates_ref, ids_ref, slots_ref, tokens_ref, out_ref):
    width = tokens_ref.shape[1]
    rows = tokens_ref.shape[0]
    columns = LANES // 2
    weighting = jnp.where(slots_ref[...] >= 0, gates_ref[...], jnp.float32(0.0))
    ids = ids_ref[...]
    column = lax.broadcasted_iota(jnp.int32, (columns, rows), 0)
    spread = jnp.zeros((columns, rows), jnp.float32)
    for k in range(ids.shape[0]):
        spread += jnp.where(ids[k : k + 1] == column, weighting[k : k + 1], jnp.float32(0.0))
    high = spread.astype(jnp.bfloat16).astype(jnp.float32)
    both = jnp.concatenate([high, spread - high], axis=0)
    out_ref[:, :width] = tokens_ref[...]
    out_ref[:, width:] = both.T.astype(jnp.bfloat16)


def pack(tokens, route_gates, expert_ids, slot_index):
    rows, width = tokens.shape
    return pl.pallas_call(
        pack_kernel,
        out_shape=jax.ShapeDtypeStruct((rows, width + LANES), jnp.bfloat16),
        cost_estimate=pl.CostEstimate(
            flops=rows * width, bytes_accessed=4 * rows * width, transcendentals=0
        ),
        name="pack",
    )(route_gates.T, expert_ids.T, slot_index.T, tokens)


def scale_kernel(*refs, pieces):
    scales, quants, out_ref = refs[:3], refs[3:6], refs[6]
    factors, held = refs[7:10], refs[10:13]
    factor_sems, sems = refs[13:]
    width, half = held[0].shape
    rows = width // pieces

    def fetch(which, piece):
        at = pl.ds(piece * rows, rows)
        return pltpu.make_async_copy(
            quants[which].at[0, at], held[which].at[at], sems.at[which, piece]
        )

    factor_copies = [
        pltpu.make_async_copy(scales[i], factors[i], factor_sems.at[i]) for i in range(3)
    ]
    for copy in factor_copies:
        copy.start()
    for piece in range(pieces):
        for which in range(3):
            fetch(which, piece).start()
    for copy in factor_copies:
        copy.wait()

    def work(piece, carry):
        for which in range(3):
            fetch(which, piece).wait()
            for i in range(rows // QB):
                for j in range(half // QB):
                    at = piece * (rows // QB) + i
                    row = pl.ds(pl.multiple_of(at * QB, QB), QB)
                    block = held[which][row, pl.ds(j * QB, QB)].astype(jnp.float32)
                    block = (block * factors[which][j, at]).astype(out_ref.dtype)
                    out_ref[row, pl.ds(which * half + j * QB, QB)] = block
        return carry

    lax.fori_loop(0, pieces, work, 0)


def scale_weights(quants, scales):
    _, width, half = quants[0].shape
    pieces = 8
    scales = [scale[0].T for scale in scales]
    return pl.pallas_call(
        functools.partial(scale_kernel, pieces=pieces),
        in_specs=[pl.BlockSpec(memory_space=pl.ANY)] * 6,
        out_specs=pl.BlockSpec(memory_space=pltpu.VMEM),
        out_shape=pltpu.VMEM((width, 3 * half), jnp.bfloat16),
        scratch_shapes=[pltpu.SMEM(scales[0].shape, jnp.float32)] * 3
        + [pltpu.VMEM((width, half), jnp.bfloat16)] * 3
        + [pltpu.SemaphoreType.DMA((3,)), pltpu.SemaphoreType.DMA((3, pieces))],
        cost_estimate=pl.CostEstimate(
            flops=3 * width * half, bytes_accessed=12 * width * half, transcendentals=0
        ),
        compiler_params=pltpu.CompilerParams(vmem_limit_bytes=52 * 2**20),
        name="scale_weights",
    )(*scales, *quants)


def contract_last(a, b):
    return lax.dot_general(a, b, (((1,), (1,)), ((), ())), preferred_element_type=jnp.float32)


def hidden_units(me, which, rows_ref, weight, half, start=0):
    width = rows_ref.shape[1] - LANES
    columns = rows_ref[start:, width:].astype(jnp.float32)
    rank = lax.rem(lax.broadcasted_iota(jnp.int32, columns.shape, 1), LANES // 2)
    gates = jnp.sum(
        jnp.where(rank == me[which], columns, jnp.float32(0.0)), axis=1, keepdims=True
    )
    tokens = rows_ref[start:, :width]
    gate_act = jnp.dot(tokens, weight[:, :half], preferred_element_type=jnp.float32)
    up_act = jnp.dot(tokens, weight[:, half : 2 * half], preferred_element_type=jnp.float32)
    return (gate_act / (1.0 + jnp.exp(-gate_act)) * up_act * gates).astype(jnp.bfloat16)


def hidden_kernel(me_ref, *refs):
    *messages, weight, out_ref, rows_ref = refs
    rows = messages[0].shape[0]
    for i, message in enumerate(messages):
        rows_ref[pl.ds(i * rows, rows), :] = message[...]
    out_ref[...] = hidden_units(me_ref, 0, rows_ref, weight, out_ref.shape[1])


def own_hidden(me, messages, weight):
    rows, columns = messages[0].shape
    total = len(messages) * rows
    width, half = columns - LANES, weight.shape[1] // 3
    vmem = pl.BlockSpec(memory_space=pltpu.VMEM)
    return pl.pallas_call(
        hidden_kernel,
        in_specs=[pl.BlockSpec(memory_space=pltpu.SMEM)] + [vmem] * (len(messages) + 1),
        out_specs=vmem,
        out_shape=pltpu.VMEM((total, half), jnp.bfloat16),
        scratch_shapes=[pltpu.VMEM((total, columns), jnp.bfloat16)],
        cost_estimate=pl.CostEstimate(
            flops=4 * total * width * half,
            bytes_accessed=4 * width * half + 2 * total * width,
            transcendentals=total * half,
        ),
        compiler_params=pltpu.CompilerParams(vmem_limit_bytes=20 * 2**20),
        name="own_hidden",
    )(me, *messages, weight)


def expert_kernel(me_ref, *refs, blocks, places, begun):
    refs = list(refs)

    def take(count):
        taken = refs[:count]
        del refs[:count]
        return taken

    messages = take(blocks)
    mine, other = take(2)
    if begun:
        before, *outs, kept, rows_ref, total_ref, sem = refs
        copy = pltpu.make_async_copy(other, kept, sem)
        copy.start()
        other = kept
    else:
        *outs, rows_ref = refs
    width = outs[0].shape[1]
    half = mine.shape[1] // 3
    row = 0
    for message in messages:
        rows_ref[pl.ds(row, message.shape[0]), :] = message[...]
        row += message.shape[0]
    if begun:
        first = hidden_units(me_ref, 0, rows_ref, mine, half, before.shape[0])
        first = jnp.concatenate([before[...], first], axis=0)
        for j in range(width // half):
            at = pl.ds(j * half, half)
            total_ref[:, at] = contract_last(first, mine[at, 2 * half :])
        copy.wait()
    else:
        first = hidden_units(me_ref, 0, rows_ref, mine, half)
    second = hidden_units(me_ref, 1, rows_ref, other, half)
    for j in range(width // half):
        at = pl.ds(j * half, half)
        answer = contract_last(second, other[at, 2 * half :])
        if begun:
            answer += total_ref[:, at]
        else:
            answer += contract_last(first, mine[at, 2 * half :])
        row = 0
        for out, place, count in places:
            part = answer[row : row + count].astype(outs[out].dtype)
            outs[out][pl.ds(place, count), at] = part
            row += count


def run_experts(me, messages, mine, other, places, before=None):
    columns = messages[0].shape[1]
    width, half = columns - LANES, mine.shape[1] // 3
    total = sum(message.shape[0] for message in messages)
    begun = before is not None
    vmem = pl.BlockSpec(memory_space=pltpu.VMEM)
    rows_out = [0] * (1 + max(out for out, _, _ in places))
    for out, _, count in places:
        rows_out[out] += count
    out_shape = [jax.ShapeDtypeStruct((n, width), jnp.bfloat16) for n in rows_out]
    scratch_shapes = [pltpu.VMEM((total, columns), jnp.bfloat16)]
    if begun:
        out_shape.append(pltpu.VMEM(other.shape, jnp.bfloat16))
        scratch_shapes.append(pltpu.VMEM((total, width), jnp.float32))
        scratch_shapes.append(pltpu.SemaphoreType.DMA)
    others = [before] if begun else []
    return list(
        pl.pallas_call(
            functools.partial(
                expert_kernel, blocks=len(messages), places=tuple(places), begun=begun
            ),
            in_specs=[pl.BlockSpec(memory_space=pltpu.SMEM)]
            + [vmem] * (len(messages) + 1)
            + [pl.BlockSpec(memory_space=pl.ANY) if begun else vmem]
            + [vmem] * len(others),
            out_specs=[vmem] * len(out_shape),
            out_shape=out_shape,
            scratch_shapes=scratch_shapes,
            cost_estimate=pl.CostEstimate(
                flops=12 * total * width * half,
                bytes_accessed=12 * width * half + 4 * total * width,
                transcendentals=2 * total * half,
            ),
            compiler_params=pltpu.CompilerParams(vmem_limit_bytes=20 * 2**20),
            name="run_experts",
        )(me, *messages, mine, other, *others)
    )


def hop(value, bit, devices):
    return lax.ppermute(value, AXES, [(i, i ^ bit) for i in range(devices)])


def after(value, *others):
    return lax.optimization_barrier((value, *others))[0]


def add(*terms):
    total = terms[0].astype(jnp.float32)
    for term in terms[1:]:
        total = total + term.astype(jnp.float32)
    return total.astype(jnp.bfloat16)


def gather_tokens(
    tokens,
    route_gates,
    expert_ids,
    slot_index,
    gate_quant,
    up_quant,
    down_quant,
    gate_scale,
    up_scale,
    down_scale,
):
    experts = lax.axis_size("expert")
    devices = experts * lax.axis_size("stream")

    def send(value, bit):
        return hop(value, bit, devices)

    core, y, z1, z2, z3, x = 1, 2, 4, 8, 12, experts
    me = lax.axis_index("expert")
    pair = jnp.stack([me, me ^ 1]).astype(jnp.int32)
    s0 = pack(tokens, route_gates, expert_ids, slot_index)
    s2 = send(s0, z2)
    x0 = send(s0, x)
    y0 = send(s0, y)
    mine = scale_weights(
        (gate_quant, up_quant, down_quant), (gate_scale, up_scale, down_scale)
    )
    swapped = send(after(mine, s2, x0, y0), core)
    s13 = send(jnp.concatenate([s0, s2]), z1)
    y2 = send(after(s2, y0), y)
    x2 = send(after(s2, x0), x)
    begun = own_hidden(pair, (x0, y0, s0, s2), mine)
    d0 = send(after(x0, s2), y)
    d2 = send(after(y2, x2, begun), x)
    x13 = send(after(s13, x2), x)
    y13 = send(after(s13, y2), y)
    d13 = send(jnp.concatenate([d0, d2]), z1)
    rows = s0.shape[0]
    x02, y02, d02, s0, s2, swapped = run_experts(
        pair,
        (x0, y0, s0, s2, x2, y2, d0, d2),
        mine,
        swapped,
        [
            (out, place * rows, rows)
            for out, place in ((0, 0), (1, 0), (3, 0), (4, 0), (0, 1), (1, 1), (2, 0), (2, 1))
        ],
        before=begun,
    )
    bx02 = send(after(x02, x13, y13), x)
    by02 = send(after(y02, y13), y)
    bd02 = send(d02, z1)
    d1, d3, x1, x3, y1, y3, s1, s3 = run_experts(
        pair, (after(d13, d02), x13, y13, s13), mine, swapped, [(i, 0, rows) for i in range(8)]
    )
    bd3 = send(after(add(d3, bd02[rows:]), bx02, by02), x)
    bd1 = send(after(add(d1, bd02[:rows]), bx02, by02), y)
    bs2 = send(after(add(s2, bx02[rows:], by02[rows:]), bd02, s3), z2)
    by1 = send(after(y1, bx02, by02, bd02), y)
    bx3 = send(after(x3, bd3), x)
    by3 = send(add(y3, bd3), y)
    bx1 = send(after(add(x1, bd1), bd3, bx3), x)
    bs3 = send(add(s3, bx3, by3), z3)
    bs1 = send(add(s1, bx1, by1), z1)
    return add(s0, bx02[:rows], by02[:rows], bs1, bs2, bs3)


def solution(mesh):
    streams = mesh.shape["stream"]
    experts = mesh.shape["expert"]

    def local(tokens, *rest):
        all_tokens = tokens.size * streams * experts
        weights = 3 * rest[3].size * streams
        move_tokens = (streams, experts) == (2, 16) and all_tokens < weights
        return (gather_tokens if move_tokens else exchange_rows)(tokens, *rest)

    return jax.shard_map(
        local,
        mesh=mesh,
        in_specs=(
            P(("stream", "expert"), None),
            P(("stream", "expert"), None),
            P(("stream", "expert"), None),
            P(("stream", "expert"), None),
            P("expert", None, "stream"),
            P("expert", None, "stream"),
            P("expert", None, "stream"),
            P("expert", None, "stream"),
            P("expert", None, "stream"),
            P("expert", None, "stream"),
        ),
        out_specs=P(("stream", "expert"), None),
        check_vma=False,
    )
```

```python
import functools

import jax
import jax.numpy as jnp
from jax import lax
from jax.experimental import pallas as pl
from jax.experimental.pallas import tpu as pltpu
from jax.sharding import PartitionSpec as P

QB = 128


def dequantize(quant, scales):
    expanded = jnp.repeat(jnp.repeat(scales, QB, axis=0), QB, axis=1)
    return (quant.astype(jnp.float32) * expanded).astype(jnp.bfloat16)


def exchange_rows(
    tokens,
    route_gates,
    expert_ids,
    slot_index,
    gate_quant,
    up_quant,
    down_quant,
    gate_scale,
    up_scale,
    down_scale,
):
    experts = lax.axis_size("expert")
    tok_rows = tokens.shape[0]
    top_count = expert_ids.shape[1]
    width = tokens.shape[1]
    capacity = max(2, tok_rows * top_count // experts)
    row_count = experts * capacity
    is_kept = slot_index >= 0
    position = jnp.where(is_kept, expert_ids * capacity + slot_index, -1)
    selector = jnp.any(
        position[None, :, :] == jnp.arange(row_count, dtype=jnp.int32)[:, None, None], axis=2
    )
    outgoing = jnp.dot(selector.astype(jnp.bfloat16), tokens, preferred_element_type=jnp.float32)
    outgoing = outgoing.astype(jnp.bfloat16).reshape(experts, capacity, width)
    incoming = lax.all_to_all(outgoing, "expert", split_axis=0, concat_axis=0, tiled=True).reshape(
        row_count, width
    )
    w_gate = dequantize(gate_quant[0], gate_scale[0])
    w_up = dequantize(up_quant[0], up_scale[0])
    w_down = dequantize(down_quant[0], down_scale[0])
    gate_piece = lax.all_gather(w_gate, "stream", axis=1, tiled=True)
    up_piece = lax.all_gather(w_up, "stream", axis=1, tiled=True)
    down_piece = lax.all_gather(w_down, "stream", axis=1, tiled=True)
    gate_act = jnp.dot(incoming, gate_piece, preferred_element_type=jnp.float32)
    up_act = jnp.dot(incoming, up_piece, preferred_element_type=jnp.float32)
    hidden = (jax.nn.silu(gate_act) * up_act).astype(jnp.bfloat16)
    running = jnp.einsum("rf,df->rd", hidden, down_piece, preferred_element_type=jnp.float32)
    expert_out = running.astype(jnp.bfloat16).reshape(experts, capacity, width)
    returned = lax.all_to_all(
        expert_out, "expert", split_axis=0, concat_axis=0, tiled=True
    ).reshape(row_count, width)
    gather_at = jnp.where(is_kept, position, 0).reshape(-1)
    picked = jnp.take(returned, gather_at, axis=0).reshape(tok_rows, top_count, width)
    weighting = jnp.where(is_kept, route_gates, jnp.float32(0.0))
    mixed_out = jnp.sum(weighting[:, :, None] * picked.astype(jnp.float32), axis=1)
    return mixed_out.astype(jnp.bfloat16)


AXES = ("stream", "expert")
LANES = 128


def pack_kernel(gates_ref, ids_ref, slots_ref, tokens_ref, out_ref):
    width = tokens_ref.shape[1]
    rows = tokens_ref.shape[0]
    columns = LANES // 2
    weighting = jnp.where(slots_ref[...] >= 0, gates_ref[...], jnp.float32(0.0))
    ids = ids_ref[...]
    column = lax.broadcasted_iota(jnp.int32, (columns, rows), 0)
    spread = jnp.zeros((columns, rows), jnp.float32)
    for k in range(ids.shape[0]):
        spread += jnp.where(ids[k : k + 1] == column, weighting[k : k + 1], jnp.float32(0.0))
    high = spread.astype(jnp.bfloat16).astype(jnp.float32)
    both = jnp.concatenate([high, spread - high], axis=0)
    out_ref[:, :width] = tokens_ref[...]
    out_ref[:, width:] = both.T.astype(jnp.bfloat16)


def pack(tokens, route_gates, expert_ids, slot_index):
    rows, width = tokens.shape
    return pl.pallas_call(
        pack_kernel,
        out_shape=jax.ShapeDtypeStruct((rows, width + LANES), jnp.bfloat16),
        cost_estimate=pl.CostEstimate(
            flops=rows * width, bytes_accessed=4 * rows * width, transcendentals=0
        ),
        name="pack",
    )(route_gates.T, expert_ids.T, slot_index.T, tokens)


def scale_kernel(*refs, pieces):
    scales, quants, out_ref = refs[:3], refs[3:6], refs[6]
    factors, held = refs[7:10], refs[10:13]
    factor_sems, sems = refs[13:]
    width, half = held[0].shape
    rows = width // pieces

    def fetch(which, piece):
        at = pl.ds(piece * rows, rows)
        return pltpu.make_async_copy(
            quants[which].at[0, at], held[which].at[at], sems.at[which, piece]
        )

    factor_copies = [
        pltpu.make_async_copy(scales[i], factors[i], factor_sems.at[i]) for i in range(3)
    ]
    for copy in factor_copies:
        copy.start()
    for piece in range(pieces):
        for which in range(3):
            fetch(which, piece).start()
    for copy in factor_copies:
        copy.wait()

    def work(piece, carry):
        for which in range(3):
            fetch(which, piece).wait()
            for i in range(rows // QB):
                for j in range(half // QB):
                    at = piece * (rows // QB) + i
                    row = pl.ds(pl.multiple_of(at * QB, QB), QB)
                    block = held[which][row, pl.ds(j * QB, QB)].astype(jnp.float32)
                    block = (block * factors[which][j, at]).astype(out_ref.dtype)
                    out_ref[row, pl.ds(which * half + j * QB, QB)] = block
        return carry

    lax.fori_loop(0, pieces, work, 0)


def scale_weights(quants, scales):
    _, width, half = quants[0].shape
    pieces = 8
    scales = [scale[0].T for scale in scales]
    return pl.pallas_call(
        functools.partial(scale_kernel, pieces=pieces),
        in_specs=[pl.BlockSpec(memory_space=pl.ANY)] * 6,
        out_specs=pl.BlockSpec(memory_space=pltpu.VMEM),
        out_shape=pltpu.VMEM((width, 3 * half), jnp.bfloat16),
        scratch_shapes=[pltpu.SMEM(scales[0].shape, jnp.float32)] * 3
        + [pltpu.VMEM((width, half), jnp.bfloat16)] * 3
        + [pltpu.SemaphoreType.DMA((3,)), pltpu.SemaphoreType.DMA((3, pieces))],
        cost_estimate=pl.CostEstimate(
            flops=3 * width * half, bytes_accessed=12 * width * half, transcendentals=0
        ),
        compiler_params=pltpu.CompilerParams(vmem_limit_bytes=52 * 2**20),
        name="scale_weights",
    )(*scales, *quants)


def contract_last(a, b):
    return lax.dot_general(a, b, (((1,), (1,)), ((), ())), preferred_element_type=jnp.float32)


def hidden_units(me, which, rows_ref, weight, half, start=0):
    width = rows_ref.shape[1] - LANES
    columns = rows_ref[start:, width:].astype(jnp.float32)
    rank = lax.rem(lax.broadcasted_iota(jnp.int32, columns.shape, 1), LANES // 2)
    gates = jnp.sum(
        jnp.where(rank == me[which], columns, jnp.float32(0.0)), axis=1, keepdims=True
    )
    tokens = rows_ref[start:, :width]
    gate_act = jnp.dot(tokens, weight[:, :half], preferred_element_type=jnp.float32)
    up_act = jnp.dot(tokens, weight[:, half : 2 * half], preferred_element_type=jnp.float32)
    return (gate_act / (1.0 + jnp.exp(-gate_act)) * up_act * gates).astype(jnp.bfloat16)


def hidden_kernel(me_ref, *refs):
    *messages, weight, out_ref, rows_ref = refs
    rows = messages[0].shape[0]
    for i, message in enumerate(messages):
        rows_ref[pl.ds(i * rows, rows), :] = message[...]
    out_ref[...] = hidden_units(me_ref, 0, rows_ref, weight, out_ref.shape[1])


def own_hidden(me, messages, weight):
    rows, columns = messages[0].shape
    total = len(messages) * rows
    width, half = columns - LANES, weight.shape[1] // 3
    vmem = pl.BlockSpec(memory_space=pltpu.VMEM)
    return pl.pallas_call(
        hidden_kernel,
        in_specs=[pl.BlockSpec(memory_space=pltpu.SMEM)] + [vmem] * (len(messages) + 1),
        out_specs=vmem,
        out_shape=pltpu.VMEM((total, half), jnp.bfloat16),
        scratch_shapes=[pltpu.VMEM((total, columns), jnp.bfloat16)],
        cost_estimate=pl.CostEstimate(
            flops=4 * total * width * half,
            bytes_accessed=4 * width * half + 2 * total * width,
            transcendentals=total * half,
        ),
        compiler_params=pltpu.CompilerParams(vmem_limit_bytes=20 * 2**20),
        name="own_hidden",
    )(me, *messages, weight)


def expert_kernel(me_ref, *refs, blocks, places, begun):
    refs = list(refs)

    def take(count):
        taken = refs[:count]
        del refs[:count]
        return taken

    messages = take(blocks)
    mine, other = take(2)
    if begun:
        before, *outs, kept, rows_ref, total_ref, sem = refs
        copy = pltpu.make_async_copy(other, kept, sem)
        copy.start()
        other = kept
    else:
        *outs, rows_ref = refs
    width = outs[0].shape[1]
    half = mine.shape[1] // 3
    row = 0
    for message in messages:
        rows_ref[pl.ds(row, message.shape[0]), :] = message[...]
        row += message.shape[0]
    if begun:
        first = hidden_units(me_ref, 0, rows_ref, mine, half, before.shape[0])
        first = jnp.concatenate([before[...], first], axis=0)
        for j in range(width // half):
            at = pl.ds(j * half, half)
            total_ref[:, at] = contract_last(first, mine[at, 2 * half :])
        copy.wait()
    else:
        first = hidden_units(me_ref, 0, rows_ref, mine, half)
    second = hidden_units(me_ref, 1, rows_ref, other, half)
    for j in range(width // half):
        at = pl.ds(j * half, half)
        answer = contract_last(second, other[at, 2 * half :])
        if begun:
            answer += total_ref[:, at]
        else:
            answer += contract_last(first, mine[at, 2 * half :])
        row = 0
        for out, place, count in places:
            part = answer[row : row + count].astype(outs[out].dtype)
            outs[out][pl.ds(place, count), at] = part
            row += count


def run_experts(me, messages, mine, other, places, before=None):
    columns = messages[0].shape[1]
    width, half = columns - LANES, mine.shape[1] // 3
    total = sum(message.shape[0] for message in messages)
    begun = before is not None
    vmem = pl.BlockSpec(memory_space=pltpu.VMEM)
    rows_out = [0] * (1 + max(out for out, _, _ in places))
    for out, _, count in places:
        rows_out[out] += count
    out_shape = [jax.ShapeDtypeStruct((n, width), jnp.bfloat16) for n in rows_out]
    scratch_shapes = [pltpu.VMEM((total, columns), jnp.bfloat16)]
    if begun:
        out_shape.append(pltpu.VMEM(other.shape, jnp.bfloat16))
        scratch_shapes.append(pltpu.VMEM((total, width), jnp.float32))
        scratch_shapes.append(pltpu.SemaphoreType.DMA)
    others = [before] if begun else []
    return list(
        pl.pallas_call(
            functools.partial(
                expert_kernel, blocks=len(messages), places=tuple(places), begun=begun
            ),
            in_specs=[pl.BlockSpec(memory_space=pltpu.SMEM)]
            + [vmem] * (len(messages) + 1)
            + [pl.BlockSpec(memory_space=pl.ANY) if begun else vmem]
            + [vmem] * len(others),
            out_specs=[vmem] * len(out_shape),
            out_shape=out_shape,
            scratch_shapes=scratch_shapes,
            cost_estimate=pl.CostEstimate(
                flops=12 * total * width * half,
                bytes_accessed=12 * width * half + 4 * total * width,
                transcendentals=2 * total * half,
            ),
            compiler_params=pltpu.CompilerParams(vmem_limit_bytes=20 * 2**20),
            name="run_experts",
        )(me, *messages, mine, other, *others)
    )


def hop(value, bit, devices):
    return lax.ppermute(value, AXES, [(i, i ^ bit) for i in range(devices)])


def after(value, *others):
    return lax.optimization_barrier((value, *others))[0]


def add(*terms):
    total = terms[0].astype(jnp.float32)
    for term in terms[1:]:
        total = total + term.astype(jnp.float32)
    return total.astype(jnp.bfloat16)


def gather_tokens(
    tokens,
    route_gates,
    expert_ids,
    slot_index,
    gate_quant,
    up_quant,
    down_quant,
    gate_scale,
    up_scale,
    down_scale,
):
    experts = lax.axis_size("expert")
    devices = experts * lax.axis_size("stream")

    def send(value, bit):
        return hop(value, bit, devices)

    core, y, z1, z2, z3, x = 1, 2, 4, 8, 12, experts
    me = lax.axis_index("expert")
    pair = jnp.stack([me, me ^ 1]).astype(jnp.int32)
    s0 = pack(tokens, route_gates, expert_ids, slot_index)
    s2 = send(s0, z2)
    x0 = send(s0, x)
    y0 = send(s0, y)
    mine = scale_weights(
        (gate_quant, up_quant, down_quant), (gate_scale, up_scale, down_scale)
    )
    swapped = send(after(mine, s2, x0, y0), core)
    s13 = send(jnp.concatenate([s0, s2]), z1)
    y2 = send(after(s2, y0), y)
    x2 = send(after(s2, x0), x)
    begun = own_hidden(pair, (x0, y0, s0, s2), mine)
    d0 = send(after(x0, s2), y)
    d2 = send(after(y2, x2, begun), x)
    x13 = send(after(s13, x2), x)
    y13 = send(after(s13, y2), y)
    d13 = send(jnp.concatenate([d0, d2]), z1)
    rows = s0.shape[0]
    x02, y02, d02, s0, s2, swapped = run_experts(
        pair,
        (x0, y0, s0, s2, x2, y2, d0, d2),
        mine,
        swapped,
        [
            (out, place * rows, rows)
            for out, place in ((0, 0), (1, 0), (3, 0), (4, 0), (0, 1), (1, 1), (2, 0), (2, 1))
        ],
        before=begun,
    )
    bx02 = send(after(x02, x13, y13), x)
    by02 = send(after(y02, y13), y)
    bd02 = send(d02, z1)
    d1, d3, x1, x3, y1, y3, s1, s3 = run_experts(
        pair, (after(d13, d02), x13, y13, s13), mine, swapped, [(i, 0, rows) for i in range(8)]
    )
    bd3 = send(after(add(d3, bd02[rows:]), bx02), x)
    bd1 = send(after(add(d1, bd02[:rows]), bx02), y)
    bs2 = send(after(add(s2, bx02[rows:], by02[rows:]), bd02, s3), z2)
    by1 = send(after(y1, bx02, by02, bd02), y)
    bx3 = send(after(x3, bd3), x)
    by3 = send(add(y3, bd3), y)
    bx1 = send(after(add(x1, bd1), bd3, bx3), x)
    bs3 = send(add(s3, bx3, by3), z3)
    bs1 = send(add(s1, bx1, by1), z1)
    return add(s0, bx02[:rows], by02[:rows], bs1, bs2, bs3)


def solution(mesh):
    streams = mesh.shape["stream"]
    experts = mesh.shape["expert"]

    def local(tokens, *rest):
        all_tokens = tokens.size * streams * experts
        weights = 3 * rest[3].size * streams
        move_tokens = (streams, experts) == (2, 16) and all_tokens < weights
        return (gather_tokens if move_tokens else exchange_rows)(tokens, *rest)

    return jax.shard_map(
        local,
        mesh=mesh,
        in_specs=(
            P(("stream", "expert"), None),
            P(("stream", "expert"), None),
            P(("stream", "expert"), None),
            P(("stream", "expert"), None),
            P("expert", None, "stream"),
            P("expert", None, "stream"),
            P("expert", None, "stream"),
            P("expert", None, "stream"),
            P("expert", None, "stream"),
            P("expert", None, "stream"),
        ),
        out_specs=P(("stream", "expert"), None),
        check_vma=False,
    )
```

```python
import functools

import jax
import jax.numpy as jnp
from jax import lax
from jax.experimental import pallas as pl
from jax.experimental.pallas import tpu as pltpu
from jax.sharding import PartitionSpec as P

QB = 128


def dequantize(quant, scales):
    expanded = jnp.repeat(jnp.repeat(scales, QB, axis=0), QB, axis=1)
    return (quant.astype(jnp.float32) * expanded).astype(jnp.bfloat16)


def exchange_rows(
    tokens,
    route_gates,
    expert_ids,
    slot_index,
    gate_quant,
    up_quant,
    down_quant,
    gate_scale,
    up_scale,
    down_scale,
):
    experts = lax.axis_size("expert")
    tok_rows = tokens.shape[0]
    top_count = expert_ids.shape[1]
    width = tokens.shape[1]
    capacity = max(2, tok_rows * top_count // experts)
    row_count = experts * capacity
    is_kept = slot_index >= 0
    position = jnp.where(is_kept, expert_ids * capacity + slot_index, -1)
    selector = jnp.any(
        position[None, :, :] == jnp.arange(row_count, dtype=jnp.int32)[:, None, None], axis=2
    )
    outgoing = jnp.dot(selector.astype(jnp.bfloat16), tokens, preferred_element_type=jnp.float32)
    outgoing = outgoing.astype(jnp.bfloat16).reshape(experts, capacity, width)
    incoming = lax.all_to_all(outgoing, "expert", split_axis=0, concat_axis=0, tiled=True).reshape(
        row_count, width
    )
    w_gate = dequantize(gate_quant[0], gate_scale[0])
    w_up = dequantize(up_quant[0], up_scale[0])
    w_down = dequantize(down_quant[0], down_scale[0])
    gate_piece = lax.all_gather(w_gate, "stream", axis=1, tiled=True)
    up_piece = lax.all_gather(w_up, "stream", axis=1, tiled=True)
    down_piece = lax.all_gather(w_down, "stream", axis=1, tiled=True)
    gate_act = jnp.dot(incoming, gate_piece, preferred_element_type=jnp.float32)
    up_act = jnp.dot(incoming, up_piece, preferred_element_type=jnp.float32)
    hidden = (jax.nn.silu(gate_act) * up_act).astype(jnp.bfloat16)
    running = jnp.einsum("rf,df->rd", hidden, down_piece, preferred_element_type=jnp.float32)
    expert_out = running.astype(jnp.bfloat16).reshape(experts, capacity, width)
    returned = lax.all_to_all(
        expert_out, "expert", split_axis=0, concat_axis=0, tiled=True
    ).reshape(row_count, width)
    gather_at = jnp.where(is_kept, position, 0).reshape(-1)
    picked = jnp.take(returned, gather_at, axis=0).reshape(tok_rows, top_count, width)
    weighting = jnp.where(is_kept, route_gates, jnp.float32(0.0))
    mixed_out = jnp.sum(weighting[:, :, None] * picked.astype(jnp.float32), axis=1)
    return mixed_out.astype(jnp.bfloat16)


AXES = ("stream", "expert")
LANES = 128


def pack_kernel(gates_ref, ids_ref, slots_ref, tokens_ref, out_ref):
    width = tokens_ref.shape[1]
    rows = tokens_ref.shape[0]
    columns = LANES // 2
    weighting = jnp.where(slots_ref[...] >= 0, gates_ref[...], jnp.float32(0.0))
    ids = ids_ref[...]
    column = lax.broadcasted_iota(jnp.int32, (columns, rows), 0)
    spread = jnp.zeros((columns, rows), jnp.float32)
    for k in range(ids.shape[0]):
        spread += jnp.where(ids[k : k + 1] == column, weighting[k : k + 1], jnp.float32(0.0))
    high = spread.astype(jnp.bfloat16).astype(jnp.float32)
    both = jnp.concatenate([high, spread - high], axis=0)
    out_ref[:, :width] = tokens_ref[...]
    out_ref[:, width:] = both.T.astype(jnp.bfloat16)


def pack(tokens, route_gates, expert_ids, slot_index):
    rows, width = tokens.shape
    return pl.pallas_call(
        pack_kernel,
        out_shape=jax.ShapeDtypeStruct((rows, width + LANES), jnp.bfloat16),
        cost_estimate=pl.CostEstimate(
            flops=rows * width, bytes_accessed=4 * rows * width, transcendentals=0
        ),
        name="pack",
    )(route_gates.T, expert_ids.T, slot_index.T, tokens)


def scale_kernel(*refs, pieces):
    scales, quants, out_ref = refs[:3], refs[3:6], refs[6]
    factors, held = refs[7:10], refs[10:13]
    factor_sems, sems = refs[13:]
    width, half = held[0].shape
    rows = width // pieces

    def fetch(which, piece):
        at = pl.ds(piece * rows, rows)
        return pltpu.make_async_copy(
            quants[which].at[0, at], held[which].at[at], sems.at[which, piece]
        )

    factor_copies = [
        pltpu.make_async_copy(scales[i], factors[i], factor_sems.at[i]) for i in range(3)
    ]
    for copy in factor_copies:
        copy.start()
    for piece in range(pieces):
        for which in range(3):
            fetch(which, piece).start()
    for copy in factor_copies:
        copy.wait()

    def work(piece, carry):
        for which in range(3):
            fetch(which, piece).wait()
            for i in range(rows // QB):
                for j in range(half // QB):
                    at = piece * (rows // QB) + i
                    row = pl.ds(pl.multiple_of(at * QB, QB), QB)
                    block = held[which][row, pl.ds(j * QB, QB)].astype(jnp.float32)
                    block = (block * factors[which][j, at]).astype(out_ref.dtype)
                    out_ref[row, pl.ds(which * half + j * QB, QB)] = block
        return carry

    lax.fori_loop(0, pieces, work, 0)


def scale_weights(quants, scales):
    _, width, half = quants[0].shape
    pieces = 8
    scales = [scale[0].T for scale in scales]
    return pl.pallas_call(
        functools.partial(scale_kernel, pieces=pieces),
        in_specs=[pl.BlockSpec(memory_space=pl.ANY)] * 6,
        out_specs=pl.BlockSpec(memory_space=pltpu.VMEM),
        out_shape=pltpu.VMEM((width, 3 * half), jnp.bfloat16),
        scratch_shapes=[pltpu.SMEM(scales[0].shape, jnp.float32)] * 3
        + [pltpu.VMEM((width, half), jnp.bfloat16)] * 3
        + [pltpu.SemaphoreType.DMA((3,)), pltpu.SemaphoreType.DMA((3, pieces))],
        cost_estimate=pl.CostEstimate(
            flops=3 * width * half, bytes_accessed=12 * width * half, transcendentals=0
        ),
        compiler_params=pltpu.CompilerParams(vmem_limit_bytes=52 * 2**20),
        name="scale_weights",
    )(*scales, *quants)


def contract_last(a, b):
    return lax.dot_general(a, b, (((1,), (1,)), ((), ())), preferred_element_type=jnp.float32)


def hidden_units(me, which, rows_ref, weight, half, start=0):
    width = rows_ref.shape[1] - LANES
    columns = rows_ref[start:, width:].astype(jnp.float32)
    rank = lax.rem(lax.broadcasted_iota(jnp.int32, columns.shape, 1), LANES // 2)
    gates = jnp.sum(
        jnp.where(rank == me[which], columns, jnp.float32(0.0)), axis=1, keepdims=True
    )
    tokens = rows_ref[start:, :width]
    gate_act = jnp.dot(tokens, weight[:, :half], preferred_element_type=jnp.float32)
    up_act = jnp.dot(tokens, weight[:, half : 2 * half], preferred_element_type=jnp.float32)
    return (gate_act / (1.0 + jnp.exp(-gate_act)) * up_act * gates).astype(jnp.bfloat16)


def hidden_kernel(me_ref, *refs):
    *messages, weight, out_ref, rows_ref = refs
    rows = messages[0].shape[0]
    for i, message in enumerate(messages):
        rows_ref[pl.ds(i * rows, rows), :] = message[...]
    out_ref[...] = hidden_units(me_ref, 0, rows_ref, weight, out_ref.shape[1])


def own_hidden(me, messages, weight):
    rows, columns = messages[0].shape
    total = len(messages) * rows
    width, half = columns - LANES, weight.shape[1] // 3
    vmem = pl.BlockSpec(memory_space=pltpu.VMEM)
    return pl.pallas_call(
        hidden_kernel,
        in_specs=[pl.BlockSpec(memory_space=pltpu.SMEM)] + [vmem] * (len(messages) + 1),
        out_specs=vmem,
        out_shape=pltpu.VMEM((total, half), jnp.bfloat16),
        scratch_shapes=[pltpu.VMEM((total, columns), jnp.bfloat16)],
        cost_estimate=pl.CostEstimate(
            flops=4 * total * width * half,
            bytes_accessed=4 * width * half + 2 * total * width,
            transcendentals=total * half,
        ),
        compiler_params=pltpu.CompilerParams(vmem_limit_bytes=20 * 2**20),
        name="own_hidden",
    )(me, *messages, weight)


def expert_kernel(me_ref, *refs, blocks, places, begun):
    refs = list(refs)

    def take(count):
        taken = refs[:count]
        del refs[:count]
        return taken

    messages = take(blocks)
    mine, other = take(2)
    if begun:
        before, *outs, kept, rows_ref, total_ref, sem = refs
        copy = pltpu.make_async_copy(other, kept, sem)
        copy.start()
        other = kept
    else:
        *outs, rows_ref = refs
    width = outs[0].shape[1]
    half = mine.shape[1] // 3
    row = 0
    for message in messages:
        rows_ref[pl.ds(row, message.shape[0]), :] = message[...]
        row += message.shape[0]
    if begun:
        first = hidden_units(me_ref, 0, rows_ref, mine, half, before.shape[0])
        first = jnp.concatenate([before[...], first], axis=0)
        for j in range(width // half):
            at = pl.ds(j * half, half)
            total_ref[:, at] = contract_last(first, mine[at, 2 * half :])
        copy.wait()
    else:
        first = hidden_units(me_ref, 0, rows_ref, mine, half)
    second = hidden_units(me_ref, 1, rows_ref, other, half)
    for j in range(width // half):
        at = pl.ds(j * half, half)
        answer = contract_last(second, other[at, 2 * half :])
        if begun:
            answer += total_ref[:, at]
        else:
            answer += contract_last(first, mine[at, 2 * half :])
        row = 0
        for out, place, count in places:
            part = answer[row : row + count].astype(outs[out].dtype)
            outs[out][pl.ds(place, count), at] = part
            row += count


def run_experts(me, messages, mine, other, places, before=None):
    columns = messages[0].shape[1]
    width, half = columns - LANES, mine.shape[1] // 3
    total = sum(message.shape[0] for message in messages)
    begun = before is not None
    vmem = pl.BlockSpec(memory_space=pltpu.VMEM)
    rows_out = [0] * (1 + max(out for out, _, _ in places))
    for out, _, count in places:
        rows_out[out] += count
    out_shape = [jax.ShapeDtypeStruct((n, width), jnp.bfloat16) for n in rows_out]
    scratch_shapes = [pltpu.VMEM((total, columns), jnp.bfloat16)]
    if begun:
        out_shape.append(pltpu.VMEM(other.shape, jnp.bfloat16))
        scratch_shapes.append(pltpu.VMEM((total, width), jnp.float32))
        scratch_shapes.append(pltpu.SemaphoreType.DMA)
    others = [before] if begun else []
    return list(
        pl.pallas_call(
            functools.partial(
                expert_kernel, blocks=len(messages), places=tuple(places), begun=begun
            ),
            in_specs=[pl.BlockSpec(memory_space=pltpu.SMEM)]
            + [vmem] * (len(messages) + 1)
            + [pl.BlockSpec(memory_space=pl.ANY) if begun else vmem]
            + [vmem] * len(others),
            out_specs=[vmem] * len(out_shape),
            out_shape=out_shape,
            scratch_shapes=scratch_shapes,
            cost_estimate=pl.CostEstimate(
                flops=12 * total * width * half,
                bytes_accessed=12 * width * half + 4 * total * width,
                transcendentals=2 * total * half,
            ),
            compiler_params=pltpu.CompilerParams(vmem_limit_bytes=20 * 2**20),
            name="run_experts",
        )(me, *messages, mine, other, *others)
    )


def hop(value, bit, devices):
    return lax.ppermute(value, AXES, [(i, i ^ bit) for i in range(devices)])


def after(value, *others):
    return lax.optimization_barrier((value, *others))[0]


def add(*terms):
    total = terms[0].astype(jnp.float32)
    for term in terms[1:]:
        total = total + term.astype(jnp.float32)
    return total.astype(jnp.bfloat16)


def gather_tokens(
    tokens,
    route_gates,
    expert_ids,
    slot_index,
    gate_quant,
    up_quant,
    down_quant,
    gate_scale,
    up_scale,
    down_scale,
):
    experts = lax.axis_size("expert")
    devices = experts * lax.axis_size("stream")

    def send(value, bit):
        return hop(value, bit, devices)

    core, y, z1, z2, z3, x = 1, 2, 4, 8, 12, experts
    me = lax.axis_index("expert")
    pair = jnp.stack([me, me ^ 1]).astype(jnp.int32)
    s0 = pack(tokens, route_gates, expert_ids, slot_index)
    s2 = send(s0, z2)
    x0 = send(s0, x)
    y0 = send(s0, y)
    mine = scale_weights(
        (gate_quant, up_quant, down_quant), (gate_scale, up_scale, down_scale)
    )
    swapped = send(after(mine, s2, x0, y0), core)
    s13 = send(jnp.concatenate([s0, s2]), z1)
    y2 = send(after(s2, y0), y)
    x2 = send(after(s2, x0), x)
    begun = own_hidden(pair, (x0, y0, s0, s2), mine)
    d0 = send(after(x0, s2), y)
    d2 = send(after(y2, x2, begun), x)
    x13 = send(after(s13, x2), x)
    y13 = send(after(s13, y2), y)
    d13 = send(jnp.concatenate([d0, d2]), z1)
    rows = s0.shape[0]
    x02, y02, d02, s0, s2, swapped = run_experts(
        pair,
        (x0, y0, s0, s2, x2, y2, d0, d2),
        mine,
        swapped,
        [
            (out, place * rows, rows)
            for out, place in ((0, 0), (1, 0), (3, 0), (4, 0), (0, 1), (1, 1), (2, 0), (2, 1))
        ],
        before=begun,
    )
    bx02 = send(after(x02, x13, y13), x)
    by02 = send(after(y02, y13), y)
    bd02 = send(d02, z1)
    d1, d3, x1, x3, y1, y3, s1, s3 = run_experts(
        pair, (after(d13, d02), x13, y13, s13), mine, swapped, [(i, 0, rows) for i in range(8)]
    )
    bd3 = send(after(add(d3, bd02[rows:]), bx02, by02), x)
    bd1 = send(after(add(d1, bd02[:rows]), bx02, by02), y)
    bs2 = send(after(add(s2, bx02[rows:], by02[rows:]), bd02, s3), z2)
    by1 = send(after(y1, bx02, by02, bd02), y)
    bx3 = send(after(x3, bd3), x)
    by3 = send(add(y3, bd3), y)
    bx1 = send(after(add(x1, bd1), bd3), x)
    bs3 = send(add(s3, bx3, by3), z3)
    bs1 = send(add(s1, bx1, by1), z1)
    return add(s0, bx02[:rows], by02[:rows], bs1, bs2, bs3)


def solution(mesh):
    streams = mesh.shape["stream"]
    experts = mesh.shape["expert"]

    def local(tokens, *rest):
        all_tokens = tokens.size * streams * experts
        weights = 3 * rest[3].size * streams
        move_tokens = (streams, experts) == (2, 16) and all_tokens < weights
        return (gather_tokens if move_tokens else exchange_rows)(tokens, *rest)

    return jax.shard_map(
        local,
        mesh=mesh,
        in_specs=(
            P(("stream", "expert"), None),
            P(("stream", "expert"), None),
            P(("stream", "expert"), None),
            P(("stream", "expert"), None),
            P("expert", None, "stream"),
            P("expert", None, "stream"),
            P("expert", None, "stream"),
            P("expert", None, "stream"),
            P("expert", None, "stream"),
            P("expert", None, "stream"),
        ),
        out_specs=P(("stream", "expert"), None),
        check_vma=False,
    )
```

```python
import functools

import jax
import jax.numpy as jnp
from jax import lax
from jax.experimental import pallas as pl
from jax.experimental.pallas import tpu as pltpu
from jax.sharding import PartitionSpec as P

QB = 128


def dequantize(quant, scales):
    expanded = jnp.repeat(jnp.repeat(scales, QB, axis=0), QB, axis=1)
    return (quant.astype(jnp.float32) * expanded).astype(jnp.bfloat16)


def exchange_rows(
    tokens,
    route_gates,
    expert_ids,
    slot_index,
    gate_quant,
    up_quant,
    down_quant,
    gate_scale,
    up_scale,
    down_scale,
):
    experts = lax.axis_size("expert")
    tok_rows = tokens.shape[0]
    top_count = expert_ids.shape[1]
    width = tokens.shape[1]
    capacity = max(2, tok_rows * top_count // experts)
    row_count = experts * capacity
    is_kept = slot_index >= 0
    position = jnp.where(is_kept, expert_ids * capacity + slot_index, -1)
    selector = jnp.any(
        position[None, :, :] == jnp.arange(row_count, dtype=jnp.int32)[:, None, None], axis=2
    )
    outgoing = jnp.dot(selector.astype(jnp.bfloat16), tokens, preferred_element_type=jnp.float32)
    outgoing = outgoing.astype(jnp.bfloat16).reshape(experts, capacity, width)
    incoming = lax.all_to_all(outgoing, "expert", split_axis=0, concat_axis=0, tiled=True).reshape(
        row_count, width
    )
    w_gate = dequantize(gate_quant[0], gate_scale[0])
    w_up = dequantize(up_quant[0], up_scale[0])
    w_down = dequantize(down_quant[0], down_scale[0])
    gate_piece = lax.all_gather(w_gate, "stream", axis=1, tiled=True)
    up_piece = lax.all_gather(w_up, "stream", axis=1, tiled=True)
    down_piece = lax.all_gather(w_down, "stream", axis=1, tiled=True)
    gate_act = jnp.dot(incoming, gate_piece, preferred_element_type=jnp.float32)
    up_act = jnp.dot(incoming, up_piece, preferred_element_type=jnp.float32)
    hidden = (jax.nn.silu(gate_act) * up_act).astype(jnp.bfloat16)
    running = jnp.einsum("rf,df->rd", hidden, down_piece, preferred_element_type=jnp.float32)
    expert_out = running.astype(jnp.bfloat16).reshape(experts, capacity, width)
    returned = lax.all_to_all(
        expert_out, "expert", split_axis=0, concat_axis=0, tiled=True
    ).reshape(row_count, width)
    gather_at = jnp.where(is_kept, position, 0).reshape(-1)
    picked = jnp.take(returned, gather_at, axis=0).reshape(tok_rows, top_count, width)
    weighting = jnp.where(is_kept, route_gates, jnp.float32(0.0))
    mixed_out = jnp.sum(weighting[:, :, None] * picked.astype(jnp.float32), axis=1)
    return mixed_out.astype(jnp.bfloat16)


AXES = ("stream", "expert")
LANES = 128


def pack_kernel(gates_ref, ids_ref, slots_ref, tokens_ref, out_ref):
    width = tokens_ref.shape[1]
    rows = tokens_ref.shape[0]
    columns = LANES // 2
    weighting = jnp.where(slots_ref[...] >= 0, gates_ref[...], jnp.float32(0.0))
    ids = ids_ref[...]
    column = lax.broadcasted_iota(jnp.int32, (columns, rows), 0)
    spread = jnp.zeros((columns, rows), jnp.float32)
    for k in range(ids.shape[0]):
        spread += jnp.where(ids[k : k + 1] == column, weighting[k : k + 1], jnp.float32(0.0))
    high = spread.astype(jnp.bfloat16).astype(jnp.float32)
    both = jnp.concatenate([high, spread - high], axis=0)
    out_ref[:, :width] = tokens_ref[...]
    out_ref[:, width:] = both.T.astype(jnp.bfloat16)


def pack(tokens, route_gates, expert_ids, slot_index):
    rows, width = tokens.shape
    return pl.pallas_call(
        pack_kernel,
        out_shape=jax.ShapeDtypeStruct((rows, width + LANES), jnp.bfloat16),
        cost_estimate=pl.CostEstimate(
            flops=rows * width, bytes_accessed=4 * rows * width, transcendentals=0
        ),
        name="pack",
    )(route_gates.T, expert_ids.T, slot_index.T, tokens)


def scale_kernel(*refs, pieces):
    scales, quants, out_ref = refs[:3], refs[3:6], refs[6]
    factors, held = refs[7:10], refs[10:13]
    factor_sems, sems = refs[13:]
    width, half = held[0].shape
    rows = width // pieces

    def fetch(which, piece):
        at = pl.ds(piece * rows, rows)
        return pltpu.make_async_copy(
            quants[which].at[0, at], held[which].at[at], sems.at[which, piece]
        )

    factor_copies = [
        pltpu.make_async_copy(scales[i], factors[i], factor_sems.at[i]) for i in range(3)
    ]
    for copy in factor_copies:
        copy.start()
    for piece in range(pieces):
        for which in range(3):
            fetch(which, piece).start()
    for copy in factor_copies:
        copy.wait()

    def work(piece, carry):
        for which in range(3):
            fetch(which, piece).wait()
            for i in range(rows // QB):
                for j in range(half // QB):
                    at = piece * (rows // QB) + i
                    row = pl.ds(pl.multiple_of(at * QB, QB), QB)
                    block = held[which][row, pl.ds(j * QB, QB)].astype(jnp.float32)
                    block = (block * factors[which][j, at]).astype(out_ref.dtype)
                    out_ref[row, pl.ds(which * half + j * QB, QB)] = block
        return carry

    lax.fori_loop(0, pieces, work, 0)


def scale_weights(quants, scales):
    _, width, half = quants[0].shape
    pieces = 8
    scales = [scale[0].T for scale in scales]
    return pl.pallas_call(
        functools.partial(scale_kernel, pieces=pieces),
        in_specs=[pl.BlockSpec(memory_space=pl.ANY)] * 6,
        out_specs=pl.BlockSpec(memory_space=pltpu.VMEM),
        out_shape=pltpu.VMEM((width, 3 * half), jnp.bfloat16),
        scratch_shapes=[pltpu.SMEM(scales[0].shape, jnp.float32)] * 3
        + [pltpu.VMEM((width, half), jnp.bfloat16)] * 3
        + [pltpu.SemaphoreType.DMA((3,)), pltpu.SemaphoreType.DMA((3, pieces))],
        cost_estimate=pl.CostEstimate(
            flops=3 * width * half, bytes_accessed=12 * width * half, transcendentals=0
        ),
        compiler_params=pltpu.CompilerParams(vmem_limit_bytes=52 * 2**20),
        name="scale_weights",
    )(*scales, *quants)


def contract_last(a, b):
    return lax.dot_general(a, b, (((1,), (1,)), ((), ())), preferred_element_type=jnp.float32)


def hidden_units(me, which, rows_ref, weight, half, start=0):
    width = rows_ref.shape[1] - LANES
    columns = rows_ref[start:, width:].astype(jnp.float32)
    rank = lax.rem(lax.broadcasted_iota(jnp.int32, columns.shape, 1), LANES // 2)
    gates = jnp.sum(
        jnp.where(rank == me[which], columns, jnp.float32(0.0)), axis=1, keepdims=True
    )
    tokens = rows_ref[start:, :width]
    gate_act = jnp.dot(tokens, weight[:, :half], preferred_element_type=jnp.float32)
    up_act = jnp.dot(tokens, weight[:, half : 2 * half], preferred_element_type=jnp.float32)
    return (gate_act / (1.0 + jnp.exp(-gate_act)) * up_act * gates).astype(jnp.bfloat16)


def hidden_kernel(me_ref, *refs):
    *messages, weight, out_ref, rows_ref = refs
    rows = messages[0].shape[0]
    for i, message in enumerate(messages):
        rows_ref[pl.ds(i * rows, rows), :] = message[...]
    out_ref[...] = hidden_units(me_ref, 0, rows_ref, weight, out_ref.shape[1])


def own_hidden(me, messages, weight):
    rows, columns = messages[0].shape
    total = len(messages) * rows
    width, half = columns - LANES, weight.shape[1] // 3
    vmem = pl.BlockSpec(memory_space=pltpu.VMEM)
    return pl.pallas_call(
        hidden_kernel,
        in_specs=[pl.BlockSpec(memory_space=pltpu.SMEM)] + [vmem] * (len(messages) + 1),
        out_specs=vmem,
        out_shape=pltpu.VMEM((total, half), jnp.bfloat16),
        scratch_shapes=[pltpu.VMEM((total, columns), jnp.bfloat16)],
        cost_estimate=pl.CostEstimate(
            flops=4 * total * width * half,
            bytes_accessed=4 * width * half + 2 * total * width,
            transcendentals=total * half,
        ),
        compiler_params=pltpu.CompilerParams(vmem_limit_bytes=20 * 2**20),
        name="own_hidden",
    )(me, *messages, weight)


def expert_kernel(me_ref, *refs, blocks, places, begun):
    refs = list(refs)

    def take(count):
        taken = refs[:count]
        del refs[:count]
        return taken

    messages = take(blocks)
    mine, other = take(2)
    if begun:
        before, *outs, kept, rows_ref, total_ref, sem = refs
        copy = pltpu.make_async_copy(other, kept, sem)
        copy.start()
        other = kept
    else:
        *outs, rows_ref = refs
    width = outs[0].shape[1]
    half = mine.shape[1] // 3
    row = 0
    for message in messages:
        rows_ref[pl.ds(row, message.shape[0]), :] = message[...]
        row += message.shape[0]
    if begun:
        first = hidden_units(me_ref, 0, rows_ref, mine, half, before.shape[0])
        first = jnp.concatenate([before[...], first], axis=0)
        for j in range(width // half):
            at = pl.ds(j * half, half)
            total_ref[:, at] = contract_last(first, mine[at, 2 * half :])
        copy.wait()
    else:
        first = hidden_units(me_ref, 0, rows_ref, mine, half)
    second = hidden_units(me_ref, 1, rows_ref, other, half)
    for j in range(width // half):
        at = pl.ds(j * half, half)
        answer = contract_last(second, other[at, 2 * half :])
        if begun:
            answer += total_ref[:, at]
        else:
            answer += contract_last(first, mine[at, 2 * half :])
        row = 0
        for out, place, count in places:
            part = answer[row : row + count].astype(outs[out].dtype)
            outs[out][pl.ds(place, count), at] = part
            row += count


def run_experts(me, messages, mine, other, places, before=None):
    columns = messages[0].shape[1]
    width, half = columns - LANES, mine.shape[1] // 3
    total = sum(message.shape[0] for message in messages)
    begun = before is not None
    vmem = pl.BlockSpec(memory_space=pltpu.VMEM)
    rows_out = [0] * (1 + max(out for out, _, _ in places))
    for out, _, count in places:
        rows_out[out] += count
    out_shape = [jax.ShapeDtypeStruct((n, width), jnp.bfloat16) for n in rows_out]
    scratch_shapes = [pltpu.VMEM((total, columns), jnp.bfloat16)]
    if begun:
        out_shape.append(pltpu.VMEM(other.shape, jnp.bfloat16))
        scratch_shapes.append(pltpu.VMEM((total, width), jnp.float32))
        scratch_shapes.append(pltpu.SemaphoreType.DMA)
    others = [before] if begun else []
    return list(
        pl.pallas_call(
            functools.partial(
                expert_kernel, blocks=len(messages), places=tuple(places), begun=begun
            ),
            in_specs=[pl.BlockSpec(memory_space=pltpu.SMEM)]
            + [vmem] * (len(messages) + 1)
            + [pl.BlockSpec(memory_space=pl.ANY) if begun else vmem]
            + [vmem] * len(others),
            out_specs=[vmem] * len(out_shape),
            out_shape=out_shape,
            scratch_shapes=scratch_shapes,
            cost_estimate=pl.CostEstimate(
                flops=12 * total * width * half,
                bytes_accessed=12 * width * half + 4 * total * width,
                transcendentals=2 * total * half,
            ),
            compiler_params=pltpu.CompilerParams(vmem_limit_bytes=20 * 2**20),
            name="run_experts",
        )(me, *messages, mine, other, *others)
    )


def hop(value, bit, devices):
    return lax.ppermute(value, AXES, [(i, i ^ bit) for i in range(devices)])


def after(value, *others):
    return lax.optimization_barrier((value, *others))[0]


def add(*terms):
    total = terms[0].astype(jnp.float32)
    for term in terms[1:]:
        total = total + term.astype(jnp.float32)
    return total.astype(jnp.bfloat16)


def gather_tokens(
    tokens,
    route_gates,
    expert_ids,
    slot_index,
    gate_quant,
    up_quant,
    down_quant,
    gate_scale,
    up_scale,
    down_scale,
):
    experts = lax.axis_size("expert")
    devices = experts * lax.axis_size("stream")

    def send(value, bit):
        return hop(value, bit, devices)

    core, y, z1, z2, z3, x = 1, 2, 4, 8, 12, experts
    me = lax.axis_index("expert")
    pair = jnp.stack([me, me ^ 1]).astype(jnp.int32)
    s0 = pack(tokens, route_gates, expert_ids, slot_index)
    s2 = send(s0, z2)
    x0 = send(s0, x)
    y0 = send(s0, y)
    mine = scale_weights(
        (gate_quant, up_quant, down_quant), (gate_scale, up_scale, down_scale)
    )
    swapped = send(after(mine, s2, x0, y0), core)
    s13 = send(jnp.concatenate([s0, s2]), z1)
    y2 = send(after(s2, y0), y)
    x2 = send(after(s2, x0), x)
    begun = own_hidden(pair, (x0, y0, s0, s2), mine)
    d0 = send(after(x0, s2), y)
    d2 = send(after(y2, x2, begun), x)
    x13 = send(after(s13, x2), x)
    y13 = send(after(s13, y2), y)
    d13 = send(jnp.concatenate([d0, d2]), z1)
    rows = s0.shape[0]
    x02, y02, d02, s0, s2, swapped = run_experts(
        pair,
        (x0, y0, s0, s2, x2, y2, d0, d2),
        mine,
        swapped,
        [
            (out, place * rows, rows)
            for out, place in ((0, 0), (1, 0), (3, 0), (4, 0), (0, 1), (1, 1), (2, 0), (2, 1))
        ],
        before=begun,
    )
    bx02 = send(after(x02, x13, y13), x)
    by02 = send(after(y02, y13), y)
    bd02 = send(d02, z1)
    d1, d3, x1, x3, y1, y3, s1, s3 = run_experts(
        pair, (after(d13, d02), x13, y13, s13), mine, swapped, [(i, 0, rows) for i in range(8)]
    )
    bd3 = send(after(add(d3, bd02[rows:]), bx02), x)
    bd1 = send(after(add(d1, bd02[:rows]), bx02), y)
    bs2 = send(after(add(s2, bx02[rows:], by02[rows:]), bd02, s3), z2)
    by1 = send(after(y1, bx02, by02, bd02), y)
    bx3 = send(after(x3, bd3), x)
    by3 = send(add(y3, bd3), y)
    bx1 = send(after(add(x1, bd1), bd3), x)
    bs3 = send(add(s3, bx3, by3), z3)
    bs1 = send(add(s1, bx1, by1), z1)
    return add(s0, bx02[:rows], by02[:rows], bs1, bs2, bs3)


def solution(mesh):
    streams = mesh.shape["stream"]
    experts = mesh.shape["expert"]

    def local(tokens, *rest):
        all_tokens = tokens.size * streams * experts
        weights = 3 * rest[3].size * streams
        move_tokens = (streams, experts) == (2, 16) and all_tokens < weights
        return (gather_tokens if move_tokens else exchange_rows)(tokens, *rest)

    return jax.shard_map(
        local,
        mesh=mesh,
        in_specs=(
            P(("stream", "expert"), None),
            P(("stream", "expert"), None),
            P(("stream", "expert"), None),
            P(("stream", "expert"), None),
            P("expert", None, "stream"),
            P("expert", None, "stream"),
            P("expert", None, "stream"),
            P("expert", None, "stream"),
            P("expert", None, "stream"),
            P("expert", None, "stream"),
        ),
        out_specs=P(("stream", "expert"), None),
        check_vma=False,
    )
```
